256 devices in a mesh: dp: 16 (over z, core), prec: 16 (over x, y).
Axes of the slice: x: 4, y: 4, z: 8, core: 2. Of those that a mesh axis runs over, the one named last changes fastest.
Arguments:
- activations: bfloat16 [4096, 8192], P('dp'), may hold values from -6 to 6
- cotangents: bfloat16 [4096, 8192], P('dp', 'prec'), may hold values from -0.09375 to 0.09375
- owner_slots: int32 [16, 16], P('dp'), may hold values from 0 to 31, as said below
- left_stats: float32 [16, 32, 512, 512], P('dp', 'prec'), as said below
- right_stats: float32 [16, 32, 512, 512], P('dp', 'prec'), as said below
Outputs:
- precond_update: bfloat16 [8192, 8192], P('dp', 'prec')
- left_fresh: float32 [16, 32, 512, 512], P('dp', 'prec')
- right_fresh: float32 [16, 32, 512, 512], P('dp', 'prec')
The draws below stay inside these ranges and needn't reach their ends.
Inputs may be any that keep to these rules, and one draw needn't show every extreme that they name: `owner_slots`: in each row the 16 blocks name distinct slots; slot q belongs to owner q // 2; an owner holds at most 2 blocks of a row and its blocks occupy its lowest slots; in every row some owner holds exactly 2. `left_stats`: every slot holds a symmetric positive definite matrix. `right_stats`: every slot holds a symmetric positive definite matrix.
All inputs are finite; a program needn't handle non-finite values. Where the reference program divides by a largest or mean magnitude, that divisor is 1e-20 or more.
Results may differ from the reference program's by a relative error of at most 0.027.
Values may be sent and summed in bfloat16 or wider, within the bound.
A program may use at most 128 MiB of HBM per device.

```python
import jax
import jax.numpy as jnp
from jax import lax

BLK = 512
ITERS = 3
CAP = 2
TOKENS = 4096
DROWS = 8192
FCOLS = 8192
N_DP = 16
N_PREC = 16


def table_row(row_key):
    part_keys = jax.random.split(row_key, 3)
    heavy_count = jax.random.randint(part_keys[0], (), 1, N_PREC // 2 + 1)
    ranking = jax.random.permutation(part_keys[1], N_PREC)
    counts = jnp.where(ranking < heavy_count, CAP, jnp.where(ranking < 2 * heavy_count, 0, 1))
    slot_ids = jnp.arange(N_PREC * CAP)
    used_slot = slot_ids % CAP < counts[slot_ids // CAP]
    scores = jnp.where(used_slot, slot_ids, slot_ids + N_PREC * CAP)
    ordered = jnp.argsort(scores)
    mixing = jax.random.permutation(part_keys[2], N_PREC)
    return ordered[:N_PREC][mixing].astype(jnp.int32)


def draw_owner_slots(key, part):
    key = jax.random.fold_in(key, 11)
    return jax.vmap(table_row)(jax.random.split(key, N_DP))


def gram_row(row_key, top_scale):
    part_keys = jax.random.split(row_key, 4)
    slot_shape = (N_PREC * CAP, BLK, BLK)
    gauss_part = jax.random.normal(part_keys[0], slot_shape, jnp.float32)
    factor = gauss_part
    gram = jnp.einsum('sik,sjk->sij', factor, factor, precision=lax.Precision.HIGHEST) / BLK
    gram = (gram + jnp.swapaxes(gram, -1, -2)) * 0.5
    ident_mat = jnp.eye(BLK, dtype=jnp.float32)
    diag_vals = jax.random.uniform(part_keys[2], slot_shape[:-1], jnp.float32, 0.35, 0.75)
    base_mat = gram + ident_mat * diag_vals[..., None]
    log_scale = jax.random.uniform(part_keys[3], slot_shape[:-1], jnp.float32, 0.0, jnp.log(top_scale))
    scales = jnp.exp(log_scale)
    return base_mat * scales[..., :, None] * scales[..., None, :]


def spd_stats(key, top_scale):
    row_keys = jax.random.split(key, N_DP)
    return lax.map(lambda row_key: gram_row(row_key, top_scale), row_keys)


def draw_left_stats(key, part):
    key = jax.random.fold_in(key, 21)
    return spd_stats(key, 3.1623)


def draw_right_stats(key, part):
    key = jax.random.fold_in(key, 22)
    return spd_stats(key, 3.1623)


def spiked(array, own_key, source, target, blocks, factor):
    owner, partner = [(jnp.arange(array.shape[dim]) // (array.shape[dim] // blocks)).reshape([-1 if axis == dim else 1 for axis in range(array.ndim)]) for dim in (source, target)]
    chosen = jax.random.permutation(own_key, blocks)[partner]
    strong = (owner == chosen) | (owner == (partner + blocks // 2) % blocks)
    return jnp.where(strong, factor * array, array)


def levels(key, extent, shards, low, largest):
    def one(axis_at, blocks):
        heights = jax.random.uniform(jax.random.fold_in(jax.random.fold_in(key, 6), axis_at), (blocks,), jnp.float32, low / len(shards), largest / len(shards))
        return jnp.repeat(jnp.exp(heights), extent[axis_at] // blocks).reshape((-1,) + (1,) * (len(extent) - axis_at - 1))

    level = one(*shards[0])
    for cut in shards[1:]:
        level = level * one(*cut)
    return level


def centred(key, dims, deviation, limit, shards=(), kind=jnp.bfloat16):
    factor_of = levels(key, dims, shards, -0.22, 0.18) if shards else 1.0
    entries = jax.random.normal(key, dims, jnp.float32) * deviation * factor_of
    return jnp.minimum(jnp.maximum(entries, -limit), limit).astype(kind)


def gaussian_with(own_key, shape, width, bound, cuts, heavy, kind=jnp.bfloat16):
    array = width * jax.random.normal(own_key, shape, jnp.float32)
    if cuts:
        array = array * levels(own_key, shape, cuts, -0.22, 0.18)
    return jnp.clip(spiked(array, jax.random.fold_in(own_key, 3), *heavy), -bound, bound).astype(kind)


def setup_inputs(seed: int = 0) -> dict:
    seeds = jax.random.split(jax.random.key(seed), 6)
    activations = gaussian_with(seeds[0], (TOKENS, DROWS), 1.0, 6.0, ((0, 16),), (0, 1, 16, 2.0))
    cotangents = centred(seeds[1], (TOKENS, FCOLS), TOKENS ** -0.5, 0.09375, ((0, 16), (1, 16)))
    owner_slots = draw_owner_slots(jax.random.fold_in(seeds[5], 71), 0)
    left_stats = draw_left_stats(jax.random.fold_in(seeds[5], 71), 0)
    right_stats = draw_right_stats(jax.random.fold_in(seeds[5], 71), 0)
    return dict(activations=activations, cotangents=cotangents, owner_slots=owner_slots, left_stats=left_stats, right_stats=right_stats)


decay_rate = 0.95

def matmul_bf(left_op, right_op):
    return jnp.dot(left_op.astype(jnp.bfloat16), right_op.astype(jnp.bfloat16), preferred_element_type=jnp.float32)

def inverse_root(matrix):
    blk_size = matrix.shape[0]
    ident_mat = jnp.eye(blk_size, dtype=jnp.float32)
    row_sum = jnp.max(lax.optimization_barrier(jnp.sum(jnp.abs(matrix), axis=1))) + 1e-06
    z_scale = 2.5 / row_sum
    moment = z_scale * matrix
    factor = (5.0 * ident_mat - moment) * 0.25
    result = jnp.sqrt(jnp.sqrt(z_scale)) * factor
    for rounds in range(1, ITERS):
        square = matmul_bf(factor, factor)
        moment = matmul_bf(square, matmul_bf(square, moment))
        factor = (5.0 * ident_mat - moment) * 0.25
        result = matmul_bf(result, factor)
    return result

def block_step(grad_block, left_old, right_old):
    blk_size = grad_block.shape[0]
    left_gram = lax.dot_general(grad_block, grad_block, (((1,), (1,)), ((), ())), preferred_element_type=jnp.float32)
    right_gram = lax.dot_general(grad_block, grad_block, (((0,), (0,)), ((), ())), preferred_element_type=jnp.float32)
    left_new = decay_rate * left_old + left_gram / blk_size
    right_new = decay_rate * right_old + right_gram / blk_size
    left_root = inverse_root(left_new)
    right_root = inverse_root(right_new)
    halfway = jnp.dot(grad_block, right_root.astype(jnp.bfloat16), preferred_element_type=jnp.float32).astype(jnp.bfloat16)
    update = jnp.dot(left_root.astype(jnp.bfloat16), halfway, preferred_element_type=jnp.float32).astype(jnp.bfloat16)
    return (left_new, right_new, update)

def reference(activations, cotangents, owner_slots, left_stats, right_stats):
    gradient = lax.dot_general(activations, cotangents, (((0,), (0,)), ((), ())), preferred_element_type=jnp.float32)
    grad_bf = gradient.astype(jnp.bfloat16)
    blocks = grad_bf.reshape(N_DP, BLK, N_PREC, BLK).transpose(0, 2, 1, 3)

    def row_step(packed):
        row_blocks, slot_ids, left_row, right_row = packed
        slot_ids = slot_ids.astype(jnp.int32)
        left_sel = left_row[slot_ids]
        right_sel = right_row[slot_ids]
        results = lax.map(lambda triple: block_step(triple[0], triple[1], triple[2]), (row_blocks, left_sel, right_sel))
        left_out = left_row.at[slot_ids].set(results[0])
        right_out = right_row.at[slot_ids].set(results[1])
        return (left_out, right_out, results[2])
    left_fresh, right_fresh, updates = lax.map(row_step, (blocks, owner_slots, left_stats, right_stats))
    precond_update = updates.transpose(0, 2, 1, 3).reshape(N_DP * BLK, N_PREC * BLK)
    return (precond_update, left_fresh, right_fresh)
```

```python
import functools

import jax
import jax.numpy as jnp
from jax import lax
from jax.experimental import pallas as pl
from jax.experimental.pallas import tpu as pltpu
from jax.sharding import PartitionSpec as P

CAP = 2
HALVES = 2
SUBS = 2
TILE = 128
UNIT = 16
DECAY = 0.95
BF = jnp.bfloat16
F32 = jnp.float32


def nn(a, b):
    return jnp.dot(a, b, preferred_element_type=F32)


def nt(a, b):
    return lax.dot_general(a, b, (((1,), (1,)), ((), ())), preferred_element_type=F32)


def tn(a, b):
    return lax.dot_general(a, b, (((0,), (0,)), ((), ())), preferred_element_type=F32)


def upper_tiles(blk):
    side = blk // TILE
    return [(i, j) for i in range(side) for j in range(i, side)]


def five_minus(m):
    rows = lax.broadcasted_iota(jnp.int32, m.shape, 0)
    cols = lax.broadcasted_iota(jnp.int32, m.shape, 1)
    return jnp.where(rows == cols, 1.25, 0.0) - 0.25 * m


def inverse_root(a_ref, out_ref, f_ref):
    a = a_ref[...]
    top = jnp.max(jnp.sum(jnp.abs(a), axis=0, keepdims=True), axis=1, keepdims=True) + 1e-06
    z = 2.5 / top
    m0 = a * z
    m0b = m0.astype(BF)
    f0b = five_minus(m0).astype(BF)
    sq = nn(f0b, f0b).astype(BF)
    quad = nn(sq, sq).astype(BF)
    f_ref[...] = five_minus(nn(quad, m0b))
    f1b = f_ref[...].astype(BF)
    s1 = nn(f1b, f1b)
    u = (5.0 * f_ref[...] - 4.0 * s1).astype(BF)
    s1 = s1.astype(BF)
    q1 = nn(s1, s1).astype(BF)
    h = (1.25 * f_ref[...] - 0.25 * nn(q1, u)).astype(BF)
    out_ref[...] = (nn(f0b, h) * jnp.sqrt(jnp.sqrt(z))).astype(BF)


def travel_kernel(
    nd, npr,
    own_ref, act_ref, cot_ref, left_ref, right_ref,
    half_ref, xr_ref, slots_ref,
    a_all, cbuf, ct, stat, pk1, st1, pk2, st2, rs_out, rs_in, part, gt, gsa, gsb, g1a, g1b, pk3a, pk3b, sla, slb, mats, f_scr, xl,
    table,
    loc_sem, stat_sem, xs, xr, rss, rsr, s1s, s1r, s2s, s2r, g1s, g1r, g2s, g2r,
):
    nz = nd // 2
    steps = nz - 1
    tok, blk = cot_ref.shape
    hrow = blk // HALVES
    drow = hrow // 2
    srow = drow // SUBS
    grow = hrow // npr
    d = lax.axis_index("dp")
    p = lax.axis_index("prec")
    z = d // 2
    core = d % 2
    twin = d + 1 - 2 * core
    up = (d + 2) % nd
    down = (d + nd - 2) % nd
    MESH = pl.DeviceIdType.MESH
    g1 = (g1a, g1b)
    gs = (gsa, gsb)
    pk3 = (pk3a, pk3b)
    landed = (sla, slb)
    tiles = upper_tiles(blk)

    def remote(src, dst, ssem, rsem, **where):
        return pltpu.make_async_remote_copy(
            src_ref=src, dst_ref=dst, send_sem=ssem, recv_sem=rsem,
            device_id=where, device_id_type=MESH,
        )

    def peers(fn):
        @pl.loop(1, npr)
        def _(s):
            fn((p + s) % npr)

    def order(k):
        if isinstance(k, int) and k == nz - 1:
            return z
        return (z + nz + (2 * (k % 2) - 1) * (k // 2 + 1)) % nz

    def own_rows(k):
        dest = order(k)
        cols = pl.ds(pl.multiple_of((2 * dest + core) * blk, blk), blk)
        return pltpu.make_async_copy(
            act_ref.at[:, cols], a_all.at[dest, pl.ds(0, tok)], loc_sem.at[k]
        )

    def twin_rows(k):
        dest = order(k)
        cols = pl.ds(pl.multiple_of((2 * dest + 1 - core) * blk, blk), blk)
        return remote(
            act_ref.at[:, cols], a_all.at[dest, pl.ds(tok, tok)], xs.at[k], xr.at[k], dp=twin
        )

    own_cot = pltpu.make_async_copy(cot_ref, cbuf.at[pl.ds(0, tok)], loc_sem.at[nz])
    twin_cot = remote(cot_ref, cbuf.at[pl.ds(tok, tok)], xs.at[nz], xr.at[nz], dp=twin)
    left_in = pltpu.make_async_copy(left_ref.at[0], stat.at[0], stat_sem.at[0])
    right_in = pltpu.make_async_copy(right_ref.at[0], stat.at[1], stat_sem.at[1])

    own_cot.start()

    @pl.loop(0, nz - 1)
    def _(k):
        own_rows(k).start()

    own_rows(nz - 1).start()
    left_in.start()
    right_in.start()

    barrier = pltpu.get_barrier_semaphore()
    for other in (twin, up, down):
        pl.semaphore_signal(barrier, inc=1, device_id={"dp": other}, device_id_type=MESH)
    peers(
        lambda t: pl.semaphore_signal(barrier, inc=1, device_id={"prec": t}, device_id_type=MESH)
    )
    pl.semaphore_wait(barrier, 3 + npr - 1)

    twin_cot.start()

    @pl.loop(0, nz - 1)
    def _(k):
        twin_rows(k).start()

    twin_rows(nz - 1).start()

    def stat_one(t):
        return remote(
            pk1.at[t], st1.at[pl.ds(p * CAP, CAP)], s1s.at[t], s1r.at[p], prec=t
        )

    def stat_one_from(u):
        return remote(
            pk1.at[u], st1.at[pl.ds(u * CAP, CAP)], s1s.at[u], s1r.at[u], prec=u
        )

    def stat_two(t):
        return remote(pk2.at[t], st2.at[p], s2s.at[t], s2r.at[p], prec=t)

    def stat_two_from(u):
        return remote(pk2.at[u], st2.at[u], s2s.at[u], s2r.at[u], prec=u)

    def pack_stats():
        left_in.wait()
        right_in.wait()

        @pl.loop(0, CAP)
        def _(slot):
            for m in range(2):
                for n, (i, j) in enumerate(tiles):
                    for u in range(TILE // UNIT):
                        at = (m * len(tiles) + n) * (TILE // UNIT) + u
                        pk1[at % npr, slot, pl.ds(at // npr * UNIT, UNIT), :] = stat[
                            m, slot, pl.ds(i * TILE + u * UNIT, UNIT), pl.ds(j * TILE, TILE)
                        ].astype(BF)

        peers(lambda t: stat_one(t).start())

    def turn_stats():
        peers(lambda u: stat_one_from(u).wait_recv())
        st1[pl.ds(p * CAP, CAP)] = pk1[p]

        @pl.loop(0, npr)
        def _(c):
            pk2[c] = st1[own_ref[0, c]]

        peers(lambda t: stat_two(t).start())

    def unpack_stats():
        peers(lambda u: stat_two_from(u).wait_recv())
        st2[p] = pk2[p]
        for m in range(2):
            for n, (i, j) in enumerate(tiles):
                rows = []
                for u in range(TILE // UNIT):
                    at = (m * len(tiles) + n) * (TILE // UNIT) + u
                    rows.append(st2[at % npr, pl.ds(at // npr * UNIT, UNIT), :])
                tile = jnp.concatenate(rows, axis=0).astype(F32) * DECAY
                mats[m, pl.ds(i * TILE, TILE), pl.ds(j * TILE, TILE)] = tile
                if i != j:
                    mats[m, pl.ds(j * TILE, TILE), pl.ds(i * TILE, TILE)] = tile.T

    def make_table():
        @pl.loop(0, npr * CAP)
        def _(q):
            def pick(c, found):
                return jnp.where(own_ref[0, c] == q, c, found)

            table[q] = lax.fori_loop(0, npr, pick, jnp.int32(0))

    def grad_one(h, t):
        return remote(
            gs[h].at[t], g1[h].at[p],
            g1s.at[h, t], g1r.at[h, p], prec=t,
        )

    def grad_one_from(h, u):
        return remote(
            gs[h].at[u], g1[h].at[u],
            g1s.at[h, u], g1r.at[h, u], prec=u,
        )

    def grad_two(h, t):
        return remote(
            pk3[h].at[t], landed[h].at[p],
            g2s.at[h, t], g2r.at[h, p], prec=t,
        )

    def grad_two_from(h, u):
        return remote(
            pk3[h].at[u], landed[h].at[u],
            g2s.at[h, u], g2r.at[h, u], prec=u,
        )

    def ring(it, way, sub):
        return remote(
            rs_out.at[it, way, sub], rs_in.at[it, way, sub],
            rss.at[it, way * SUBS + sub], rsr.at[it, way * SUBS + sub],
            dp=up if way == 0 else down,
        )

    def finish_half(h):
        base = h * hrow
        last = h * steps + steps - 1
        for way in range(2):
            rows = pl.ds(base + way * drow, drow)
            part[way] = nn(ct[rows, :], a_all[z])
            for sub in range(SUBS):
                ring(last, way, sub).wait_recv()
                done = (
                    part[way, pl.ds(sub * srow, srow), :] + rs_in[last, way, sub].astype(F32)
                ).astype(BF)
                gt[pl.ds(base + way * drow + sub * srow, srow), :] = done
                first = (way * drow + sub * srow) // grow
                gs[h][pl.ds(first, srow // grow)] = done.reshape(srow // grow, grow, blk)
        peers(lambda t: grad_one(h, t).start())

    def turn_half(h):
        peers(lambda u: grad_one_from(h, u).wait_recv())
        g1[h][p] = gs[h][p]

        @pl.loop(0, npr)
        def _(o):
            for slot in range(CAP):
                pk3[h][o, slot] = g1[h][table[o * CAP + slot]]

        peers(lambda t: grad_two(h, t).start())

    own_cot.wait()
    twin_cot.wait_recv()
    ct[...] = cbuf[...].T

    @pl.loop(0, nz - 1)
    def _(k):
        own_rows(k).wait()
        twin_rows(k).wait_recv()

    own_rows(nz - 1).wait()
    twin_rows(nz - 1).wait_recv()

    @pl.loop(0, HALVES * steps)
    def _(it):
        h = it // steps
        s = it % steps

        for way in range(2):
            dest = (z + nz - 1 - s) % nz if way == 0 else (z + 1 + s) % nz
            rows = pl.ds(pl.multiple_of(h * hrow + way * drow, drow), drow)
            part[way] = nn(ct[rows, :], a_all[dest])
        for sub in range(SUBS):
            for way in range(2):
                rows = pl.ds(sub * srow, srow)

                @pl.when(s == 0)
                def _():
                    rs_out[it, way, sub] = part[way, rows, :].astype(BF)

                @pl.when(s > 0)
                def _():
                    ring(it - 1, way, sub).wait_recv()
                    rs_out[it, way, sub] = (
                        part[way, rows, :] + rs_in[it - 1, way, sub].astype(F32)
                    ).astype(BF)

                ring(it, way, sub).start()

        @pl.when(it == 0)
        def _():
            pack_stats()

        @pl.when(it == 1)
        def _():
            make_table()

        @pl.when(it == steps)
        def _():
            finish_half(0)

        @pl.when(it == steps + 1)
        def _():
            turn_stats()

        @pl.when(it == steps + steps // 2)
        def _():
            turn_half(0)

        @pl.when(it == 2 * steps - 1)
        def _():
            unpack_stats()

    finish_half(1)
    g = gt[...]
    mats[1] += nt(g, g) * (1.0 / blk)
    inverse_root(mats.at[1], xr_ref, f_scr)
    turn_half(1)
    mats[0] += tn(g, g) * (1.0 / blk)
    inverse_root(mats.at[0], xl, f_scr)
    half_ref[...] = nt(xl[...], gt[...]).astype(BF)

    for h in range(HALVES):
        peers(lambda u, h=h: grad_two_from(h, u).wait_recv())
        landed[h][p] = pk3[h][p]
        slots_ref[h] = landed[h][...]

    twin_cot.wait_send()

    @pl.loop(0, nz - 1)
    def _(k):
        twin_rows(k).wait_send()

    twin_rows(nz - 1).wait_send()

    @pl.loop(0, HALVES * steps)
    def _(it):
        for way in range(2):
            for sub in range(SUBS):
                ring(it, way, sub).wait_send()

    def sent(t):
        stat_one(t).wait_send()
        stat_two(t).wait_send()
        for h in range(HALVES):
            grad_one(h, t).wait_send()
            grad_two(h, t).wait_send()

    peers(sent)


def fresh_kernel(parts, own_ref, half_ref, xr_ref, slots_ref, left_ref, right_ref,
                 upd_ref, lout_ref, rout_ref, g_scr):
    step = pl.program_id(0)
    slot = step // parts
    piece = step % parts
    blk = half_ref.shape[0]
    rows = blk // parts
    q = lax.axis_index("prec") * CAP + slot
    named = jnp.int32(0)
    for c in range(own_ref.shape[1]):
        named = named + (own_ref[0, c] == q).astype(jnp.int32)

    @pl.when(step == 0)
    def _():
        upd_ref[...] = nn(half_ref[...], xr_ref[...]).astype(BF)

    @pl.when(named > 0)
    def _():
        at = pl.multiple_of(piece * rows, rows)
        g = slots_ref[...].reshape(blk, blk)
        g_scr[...] = g
        lout_ref[0, 0] = DECAY * left_ref[0, 0] + tn(g_scr[:, pl.ds(at, rows)], g) * (1.0 / blk)
        rout_ref[0, 0] = DECAY * right_ref[0, 0] + nt(g_scr[pl.ds(at, rows), :], g) * (1.0 / blk)

    @pl.when(named == 0)
    def _():
        lout_ref[...] = left_ref[...]
        rout_ref[...] = right_ref[...]


def shards(activations, cotangents, owner_slots, left_stats, right_stats):
    nd = lax.axis_size("dp")
    npr = lax.axis_size("prec")
    tok, blk = cotangents.shape
    nz = nd // 2
    its = HALVES * (nz - 1)
    hrow = blk // HALVES
    srow = hrow // 2 // SUBS
    grow = hrow // npr
    srows = 2 * len(upper_tiles(blk)) * TILE // npr
    dma = pltpu.SemaphoreType.DMA
    vmem = pl.BlockSpec(memory_space=pltpu.VMEM)
    far = pl.BlockSpec(memory_space=pltpu.HBM)
    half, xr, slots = pl.pallas_call(
        functools.partial(travel_kernel, nd, npr),
        out_shape=[
            jax.ShapeDtypeStruct((blk, blk), BF),
            jax.ShapeDtypeStruct((blk, blk), BF),
            jax.ShapeDtypeStruct((HALVES, npr, CAP, grow, blk), BF),
        ],
        in_specs=[pl.BlockSpec(memory_space=pltpu.SMEM)] + [far] * 4,
        out_specs=[vmem] * 3,
        scratch_shapes=[
            pltpu.VMEM((nz, 2 * tok, blk), BF),
            pltpu.VMEM((2 * tok, blk), BF),
            pltpu.VMEM((blk, 2 * tok), BF),
            pltpu.VMEM((2, CAP, blk, blk), F32),
            pltpu.VMEM((npr, CAP, srows, TILE), BF),
            pltpu.VMEM((npr * CAP, srows, TILE), BF),
            pltpu.VMEM((npr, srows, TILE), BF),
            pltpu.VMEM((npr, srows, TILE), BF),
            pltpu.VMEM((its, 2, SUBS, srow, blk), BF),
            pltpu.VMEM((its, 2, SUBS, srow, blk), BF),
            pltpu.VMEM((2, hrow // 2, blk), F32),
            pltpu.VMEM((blk, blk), BF),
            pltpu.VMEM((npr, grow, blk), BF),
            pltpu.VMEM((npr, grow, blk), BF),
            pltpu.VMEM((npr, grow, blk), BF),
            pltpu.VMEM((npr, grow, blk), BF),
            pltpu.VMEM((npr, CAP, grow, blk), BF),
            pltpu.VMEM((npr, CAP, grow, blk), BF),
            pltpu.VMEM((npr, CAP, grow, blk), BF),
            pltpu.VMEM((npr, CAP, grow, blk), BF),
            pltpu.VMEM((2, blk, blk), F32),
            pltpu.VMEM((blk, blk), F32),
            pltpu.VMEM((blk, blk), BF),
            pltpu.SMEM((npr * CAP,), jnp.int32),
            dma((nz + 1,)),
            dma((2,)),
            dma((nz + 1,)),
            dma((nz + 1,)),
            dma((its, 2 * SUBS)),
            dma((its, 2 * SUBS)),
            dma((npr,)),
            dma((npr,)),
            dma((npr,)),
            dma((npr,)),
            dma((HALVES, npr)),
            dma((HALVES, npr)),
            dma((HALVES, npr)),
            dma((HALVES, npr)),
        ],
        compiler_params=pltpu.CompilerParams(
            collective_id=0, has_side_effects=True, vmem_limit_bytes=60 * 1024 * 1024
        ),
        name="travel",
    )(owner_slots, activations, cotangents, left_stats, right_stats)

    parts = 2
    rows = blk // parts
    stat_spec = pl.BlockSpec((1, 1, rows, blk), lambda i: (0, i // parts, i % parts, 0))
    whole = pl.BlockSpec((blk, blk), lambda i: (0, 0))
    update, left_out, right_out = pl.pallas_call(
        functools.partial(fresh_kernel, parts),
        grid=(CAP * parts,),
        out_shape=[
            jax.ShapeDtypeStruct((blk, blk), BF),
            jax.ShapeDtypeStruct(left_stats.shape, F32),
            jax.ShapeDtypeStruct(right_stats.shape, F32),
        ],
        in_specs=[
            pl.BlockSpec(memory_space=pltpu.SMEM),
            whole,
            whole,
            pl.BlockSpec((HALVES, npr, 1, grow, blk), lambda i: (0, 0, i // parts, 0, 0)),
            stat_spec,
            stat_spec,
        ],
        out_specs=[whole, stat_spec, stat_spec],
        scratch_shapes=[pltpu.VMEM((blk, blk), BF)],
        compiler_params=pltpu.CompilerParams(vmem_limit_bytes=60 * 1024 * 1024),
        name="fresh",
    )(owner_slots, half, xr, slots, left_stats, right_stats)
    return (update, left_out, right_out)


def solution(mesh):
    placed = (
        P("dp", None),
        P("dp", "prec"),
        P("dp", None),
        P("dp", "prec", None, None),
        P("dp", "prec", None, None),
    )
    return jax.shard_map(
        shards,
        mesh=mesh,
        in_specs=placed,
        out_specs=(P("dp", "prec"), P("dp", "prec", None, None), P("dp", "prec", None, None)),
        check_vma=False,
    )
```

```python
import functools

import jax
import jax.numpy as jnp
from jax import lax
from jax.experimental import pallas as pl
from jax.experimental.pallas import tpu as pltpu
from jax.sharding import PartitionSpec as P

CAP = 2
HALVES = 2
SUBS = 2
TILE = 128
UNIT = 16
DECAY = 0.95
BF = jnp.bfloat16
F32 = jnp.float32


def nn(a, b):
    return jnp.dot(a, b, preferred_element_type=F32)


def nt(a, b):
    return lax.dot_general(a, b, (((1,), (1,)), ((), ())), preferred_element_type=F32)


def tn(a, b):
    return lax.dot_general(a, b, (((0,), (0,)), ((), ())), preferred_element_type=F32)


def upper_tiles(blk):
    side = blk // TILE
    return [(i, j) for i in range(side) for j in range(i, side)]


def five_minus(m):
    rows = lax.broadcasted_iota(jnp.int32, m.shape, 0)
    cols = lax.broadcasted_iota(jnp.int32, m.shape, 1)
    return jnp.where(rows == cols, 1.25, 0.0) - 0.25 * m


def inverse_root(a_ref, out_ref, f_ref):
    a = a_ref[...]
    top = jnp.max(jnp.sum(jnp.abs(a), axis=0, keepdims=True), axis=1, keepdims=True) + 1e-06
    z = 2.5 / top
    m0 = a * z
    m0b = m0.astype(BF)
    f0b = five_minus(m0).astype(BF)
    sq = nn(f0b, f0b).astype(BF)
    quad = nn(sq, sq).astype(BF)
    f_ref[...] = five_minus(nn(quad, m0b))
    f1b = f_ref[...].astype(BF)
    s1 = nn(f1b, f1b)
    u = (5.0 * f_ref[...] - 4.0 * s1).astype(BF)
    s1 = s1.astype(BF)
    q1 = nn(s1, s1).astype(BF)
    h = (1.25 * f_ref[...] - 0.25 * nn(q1, u)).astype(BF)
    out_ref[...] = (nn(f0b, h) * jnp.sqrt(jnp.sqrt(z))).astype(BF)


def travel_kernel(
    nd, npr,
    own_ref, act_ref, cot_ref, left_ref, right_ref,
    half_ref, xr_ref, slots_ref,
    a_all, cbuf, ct, stat, pk1, st1, pk2, st2, rs_out, rs_in, part, gt, gsa, gsb, g1a, g1b, pk3a, pk3b, sla, slb, mats, f_scr, xl,
    table,
    loc_sem, stat_sem, xs, xr, rss, rsr, s1s, s1r, s2s, s2r, g1s, g1r, g2s, g2r,
):
    nz = nd // 2
    arc = nz // 2
    tok, blk = cot_ref.shape
    hrow = blk // HALVES
    srow = hrow // SUBS
    grow = hrow // npr
    d = lax.axis_index("dp")
    p = lax.axis_index("prec")
    z = d // 2
    core = d % 2
    twin = d + 1 - 2 * core
    up = (d + 2) % nd
    down = (d + nd - 2) % nd
    MESH = pl.DeviceIdType.MESH
    g1 = (g1a, g1b)
    gs = (gsa, gsb)
    pk3 = (pk3a, pk3b)
    landed = (sla, slb)
    tiles = upper_tiles(blk)

    def remote(src, dst, ssem, rsem, **where):
        return pltpu.make_async_remote_copy(
            src_ref=src, dst_ref=dst, send_sem=ssem, recv_sem=rsem,
            device_id=where, device_id_type=MESH,
        )

    def peers(fn):
        @pl.loop(1, npr)
        def _(s):
            fn((p + s) % npr)

    def order(k):
        return (z + nz + (2 * (k % 2) - 1) * (arc - (k + 1) // 2)) % nz

    def own_rows(k):
        dest = order(k)
        cols = pl.ds(pl.multiple_of((2 * dest + core) * blk, blk), blk)
        return pltpu.make_async_copy(
            act_ref.at[:, cols], a_all.at[k, pl.ds(0, tok)], loc_sem.at[k]
        )

    def twin_rows(k):
        dest = order(k)
        cols = pl.ds(pl.multiple_of((2 * dest + 1 - core) * blk, blk), blk)
        return remote(
            act_ref.at[:, cols], a_all.at[k, pl.ds(tok, tok)], xs.at[k], xr.at[k], dp=twin
        )

    own_cot = pltpu.make_async_copy(cot_ref, cbuf.at[pl.ds(0, tok)], loc_sem.at[nz])
    twin_cot = remote(cot_ref, cbuf.at[pl.ds(tok, tok)], xs.at[nz], xr.at[nz], dp=twin)
    left_in = pltpu.make_async_copy(left_ref.at[0], stat.at[0], stat_sem.at[0])
    right_in = pltpu.make_async_copy(right_ref.at[0], stat.at[1], stat_sem.at[1])

    def make_table():
        @pl.loop(0, npr * CAP)
        def _(q):
            def pick(c, found):
                return jnp.where(own_ref[0, c] == q, c, found)

            table[q] = lax.fori_loop(0, npr, pick, jnp.int32(0))

    own_cot.start()

    @pl.loop(0, nz)
    def _(k):
        own_rows(k).start()

    left_in.start()
    right_in.start()

    barrier = pltpu.get_barrier_semaphore()
    for other in (twin, up, down):
        pl.semaphore_signal(barrier, inc=1, device_id={"dp": other}, device_id_type=MESH)
    peers(
        lambda t: pl.semaphore_signal(barrier, inc=1, device_id={"prec": t}, device_id_type=MESH)
    )
    make_table()
    pl.semaphore_wait(barrier, 3 + npr - 1)

    twin_cot.start()

    @pl.loop(0, nz)
    def _(k):
        twin_rows(k).start()

    def stat_one(t):
        return remote(
            pk1.at[t], st1.at[pl.ds(p * CAP, CAP)], s1s.at[t], s1r.at[p], prec=t
        )

    def stat_one_from(u):
        return remote(
            pk1.at[u], st1.at[pl.ds(u * CAP, CAP)], s1s.at[u], s1r.at[u], prec=u
        )

    def stat_two(t):
        return remote(pk2.at[t], st2.at[p], s2s.at[t], s2r.at[p], prec=t)

    def stat_two_from(u):
        return remote(pk2.at[u], st2.at[u], s2s.at[u], s2r.at[u], prec=u)

    def pack_stats():
        left_in.wait()
        right_in.wait()

        @pl.loop(0, CAP)
        def _(slot):
            for m in range(2):
                for n, (i, j) in enumerate(tiles):
                    for u in range(TILE // UNIT):
                        at = (m * len(tiles) + n) * (TILE // UNIT) + u
                        pk1[at % npr, slot, pl.ds(at // npr * UNIT, UNIT), :] = stat[
                            m, slot, pl.ds(i * TILE + u * UNIT, UNIT), pl.ds(j * TILE, TILE)
                        ].astype(BF)

    def turn_stats():
        peers(lambda u: stat_one_from(u).wait_recv())
        st1[pl.ds(p * CAP, CAP)] = pk1[p]

        @pl.loop(0, npr)
        def _(c):
            pk2[c] = st1[own_ref[0, c]]

        peers(lambda t: stat_two(t).start())

    def unpack_stats():
        peers(lambda u: stat_two_from(u).wait_recv())
        st2[p] = pk2[p]
        for m in range(2):
            for n, (i, j) in enumerate(tiles):
                rows = []
                for u in range(TILE // UNIT):
                    at = (m * len(tiles) + n) * (TILE // UNIT) + u
                    rows.append(st2[at % npr, pl.ds(at // npr * UNIT, UNIT), :])
                tile = jnp.concatenate(rows, axis=0).astype(F32) * DECAY
                mats[m, pl.ds(i * TILE, TILE), pl.ds(j * TILE, TILE)] = tile
                if i != j:
                    mats[m, pl.ds(j * TILE, TILE), pl.ds(i * TILE, TILE)] = tile.T

    def grad_one(h, t):
        return remote(
            gs[h].at[t], g1[h].at[p],
            g1s.at[h, t], g1r.at[h, p], prec=t,
        )

    def grad_one_from(h, u):
        return remote(
            gs[h].at[u], g1[h].at[u],
            g1s.at[h, u], g1r.at[h, u], prec=u,
        )

    def grad_two(h, t):
        return remote(
            pk3[h].at[t], landed[h].at[p],
            g2s.at[h, t], g2r.at[h, p], prec=t,
        )

    def grad_two_from(h, u):
        return remote(
            pk3[h].at[u], landed[h].at[u],
            g2s.at[h, u], g2r.at[h, u], prec=u,
        )

    def ring(it, way, sub):
        return remote(
            rs_out.at[it, way, sub], rs_in.at[it, way, sub],
            rss.at[it, way * SUBS + sub], rsr.at[it, way * SUBS + sub],
            dp=up if way == 0 else down,
        )

    def finish_half(h):
        base = h * hrow
        last = h * arc + arc - 1
        part[0] = nn(ct[pl.ds(base, hrow), :], a_all[nz - 1])
        for sub in range(SUBS):
            for way in range(2):
                ring(last, way, sub).wait_recv()
            done = (
                part[0, pl.ds(sub * srow, srow), :]
                + rs_in[last, 0, sub].astype(F32)
                + rs_in[last, 1, sub].astype(F32)
            ).astype(BF)
            gt[pl.ds(base + sub * srow, srow), :] = done
            gs[h][pl.ds(sub * srow // grow, srow // grow)] = done.reshape(
                srow // grow, grow, blk
            )
        peers(lambda t: grad_one(h, t).start())

    def turn_half(h):
        peers(lambda u: grad_one_from(h, u).wait_recv())
        g1[h][p] = gs[h][p]

        @pl.loop(0, npr)
        def _(o):
            for slot in range(CAP):
                pk3[h][o, slot] = g1[h][table[o * CAP + slot]]

        peers(lambda t: grad_two(h, t).start())

    def rows_ready(k):
        own_rows(k).wait()
        twin_rows(k).wait_recv()

    def far_end(way, sub):
        return (way == 0) == (sub < SUBS // 2)

    lanes = [(way, sub) for sub in range(SUBS) for way in range(2)]
    lanes.sort(key=lambda lane: far_end(*lane))

    def ring_step(h, s):
        it = h * arc + s
        mine = pl.ds(h * hrow, hrow)

        @pl.when(s == 0)
        def _():
            part[0] = nn(ct[mine, :], a_all[0])

        @pl.when(s > 0)
        def _():
            part[0] = nn(ct[mine, :], a_all[2 * s - 1])
            part[1] = nn(ct[mine, :], a_all[2 * s])

        for way, sub in lanes:
            rows = pl.ds(sub * srow, srow)
            begin = 0 if far_end(way, sub) else 1

            @pl.when(s == begin)
            def _():
                rs_out[it, way, sub] = part[begin * way, rows, :].astype(BF)
                ring(it, way, sub).start()

            @pl.when(s > begin)
            def _():
                ring(it - 1, way, sub).wait_recv()
                rs_out[it, way, sub] = (
                    part[way, rows, :] + rs_in[it - 1, way, sub].astype(F32)
                ).astype(BF)
                ring(it, way, sub).start()

    pack_stats()
    own_cot.wait()
    twin_cot.wait_recv()
    ct[...] = cbuf[...].T

    @pl.loop(0, arc)
    def _(s):
        @pl.when(s > 0)
        def _():
            rows_ready(2 * s - 1)

        rows_ready(2 * s)
        for h in range(HALVES):
            ring_step(h, s)

        @pl.when(s == 0)
        def _():
            peers(lambda t: stat_one(t).start())

        @pl.when(s == arc - 2)
        def _():
            turn_stats()

    rows_ready(nz - 1)
    finish_half(0)
    unpack_stats()
    turn_half(0)
    finish_half(1)
    g = gt[...]
    mats[1] += nt(g, g) * (1.0 / blk)
    inverse_root(mats.at[1], xr_ref, f_scr)
    turn_half(1)
    mats[0] += tn(g, g) * (1.0 / blk)
    inverse_root(mats.at[0], xl, f_scr)
    half_ref[...] = nt(xl[...], gt[...]).astype(BF)

    for h in range(HALVES):
        peers(lambda u, h=h: grad_two_from(h, u).wait_recv())
        landed[h][p] = pk3[h][p]
        slots_ref[h] = landed[h][...]

    twin_cot.wait_send()

    @pl.loop(0, nz)
    def _(k):
        twin_rows(k).wait_send()

    @pl.loop(0, HALVES * arc)
    def _(it):
        for way, sub in lanes:
            if far_end(way, sub):
                ring(it, way, sub).wait_send()
            else:

                @pl.when(it % arc > 0)
                def _():
                    ring(it, way, sub).wait_send()

    def sent(t):
        stat_one(t).wait_send()
        stat_two(t).wait_send()
        for h in range(HALVES):
            grad_one(h, t).wait_send()
            grad_two(h, t).wait_send()

    peers(sent)


def fresh_kernel(own_ref, half_ref, xr_ref, slots_ref, left_ref, right_ref,
                 upd_ref, lout_ref, rout_ref, stat, g_scr, half, xr, upd, in_sem, out_sem):
    blk = xr.shape[0]
    first = lax.axis_index("prec") * CAP
    stats_in, stats_out = (left_ref, right_ref), (lout_ref, rout_ref)
    slabs = slots_ref.shape[1]
    grow = slots_ref.shape[3]

    def fetch(slot, m):
        return pltpu.make_async_copy(
            stats_in[m].at[0, slot], stat.at[slot, m], in_sem.at[slot * 2 + m]
        )

    def store(slot, m):
        return pltpu.make_async_copy(
            stat.at[slot, m], stats_out[m].at[0, slot], out_sem.at[slot * 2 + m]
        )

    def block(slot):
        return pltpu.make_async_copy(
            slots_ref.at[:, :, slot], g_scr.at[slot], in_sem.at[2 * CAP + slot]
        )

    half_in = pltpu.make_async_copy(half_ref, half, in_sem.at[3 * CAP])
    xr_in = pltpu.make_async_copy(xr_ref, xr, in_sem.at[3 * CAP + 1])
    upd_out = pltpu.make_async_copy(upd, upd_ref, out_sem.at[2 * CAP])

    for slot in range(CAP):
        block(slot).start()
        fetch(slot, 0).start()
        fetch(slot, 1).start()
    half_in.start()
    xr_in.start()
    for slot in range(CAP):
        named = jnp.int32(0)
        for c in range(own_ref.shape[1]):
            named = named + (own_ref[0, c] == first + slot).astype(jnp.int32)
        block(slot).wait()
        for m, product in ((1, nt), (0, tn)):
            fetch(slot, m).wait()

            @pl.when(named > 0)
            def _():
                g = g_scr[slot].reshape(HALVES * slabs * grow, blk)
                stat[slot, m] = DECAY * stat[slot, m] + product(g, g) * (1.0 / blk)

            store(slot, m).start()
    half_in.wait()
    xr_in.wait()
    upd[...] = nn(half[...], xr[...]).astype(BF)
    upd_out.start()
    for slot in range(CAP):
        for m in range(2):
            store(slot, m).wait()
    upd_out.wait()


def shards(activations, cotangents, owner_slots, left_stats, right_stats):
    nd = lax.axis_size("dp")
    npr = lax.axis_size("prec")
    tok, blk = cotangents.shape
    nz = nd // 2
    its = HALVES * (nz // 2)
    hrow = blk // HALVES
    srow = hrow // SUBS
    grow = hrow // npr
    srows = 2 * len(upper_tiles(blk)) * TILE // npr
    dma = pltpu.SemaphoreType.DMA
    vmem = pl.BlockSpec(memory_space=pltpu.VMEM)
    far = pl.BlockSpec(memory_space=pltpu.HBM)
    half, xr, slots = pl.pallas_call(
        functools.partial(travel_kernel, nd, npr),
        out_shape=[
            jax.ShapeDtypeStruct((blk, blk), BF),
            jax.ShapeDtypeStruct((blk, blk), BF),
            jax.ShapeDtypeStruct((HALVES, npr, CAP, grow, blk), BF),
        ],
        in_specs=[pl.BlockSpec(memory_space=pltpu.SMEM)] + [far] * 4,
        out_specs=[vmem] * 3,
        scratch_shapes=[
            pltpu.VMEM((nz, 2 * tok, blk), BF),
            pltpu.VMEM((2 * tok, blk), BF),
            pltpu.VMEM((blk, 2 * tok), BF),
            pltpu.VMEM((2, CAP, blk, blk), F32),
            pltpu.VMEM((npr, CAP, srows, TILE), BF),
            pltpu.VMEM((npr * CAP, srows, TILE), BF),
            pltpu.VMEM((npr, srows, TILE), BF),
            pltpu.VMEM((npr, srows, TILE), BF),
            pltpu.VMEM((its, 2, SUBS, srow, blk), BF),
            pltpu.VMEM((its, 2, SUBS, srow, blk), BF),
            pltpu.VMEM((2, hrow, blk), F32),
            pltpu.VMEM((blk, blk), BF),
            pltpu.VMEM((npr, grow, blk), BF),
            pltpu.VMEM((npr, grow, blk), BF),
            pltpu.VMEM((npr, grow, blk), BF),
            pltpu.VMEM((npr, grow, blk), BF),
            pltpu.VMEM((npr, CAP, grow, blk), BF),
            pltpu.VMEM((npr, CAP, grow, blk), BF),
            pltpu.VMEM((npr, CAP, grow, blk), BF),
            pltpu.VMEM((npr, CAP, grow, blk), BF),
            pltpu.VMEM((2, blk, blk), F32),
            pltpu.VMEM((blk, blk), F32),
            pltpu.VMEM((blk, blk), BF),
            pltpu.SMEM((npr * CAP,), jnp.int32),
            dma((nz + 1,)),
            dma((2,)),
            dma((nz + 1,)),
            dma((nz + 1,)),
            dma((its, 2 * SUBS)),
            dma((its, 2 * SUBS)),
            dma((npr,)),
            dma((npr,)),
            dma((npr,)),
            dma((npr,)),
            dma((HALVES, npr)),
            dma((HALVES, npr)),
            dma((HALVES, npr)),
            dma((HALVES, npr)),
        ],
        compiler_params=pltpu.CompilerParams(
            collective_id=0, has_side_effects=True, vmem_limit_bytes=60 * 1024 * 1024
        ),
        name="travel",
    )(owner_slots, activations, cotangents, left_stats, right_stats)

    update, left_out, right_out = pl.pallas_call(
        fresh_kernel,
        out_shape=[
            jax.ShapeDtypeStruct((blk, blk), BF),
            jax.ShapeDtypeStruct(left_stats.shape, F32),
            jax.ShapeDtypeStruct(right_stats.shape, F32),
        ],
        in_specs=[pl.BlockSpec(memory_space=pltpu.SMEM)] + [far] * 5,
        out_specs=[far] * 3,
        scratch_shapes=[
            pltpu.VMEM((CAP, 2, blk, blk), F32),
            pltpu.VMEM((CAP, HALVES, npr, grow, blk), BF),
            pltpu.VMEM((blk, blk), BF),
            pltpu.VMEM((blk, blk), BF),
            pltpu.VMEM((blk, blk), BF),
            dma((3 * CAP + 2,)),
            dma((2 * CAP + 1,)),
        ],
        compiler_params=pltpu.CompilerParams(vmem_limit_bytes=60 * 1024 * 1024),
        name="fresh",
    )(owner_slots, half, xr, slots, left_stats, right_stats)
    return (update, left_out, right_out)


def solution(mesh):
    placed = (
        P("dp", None),
        P("dp", "prec"),
        P("dp", None),
        P("dp", "prec", None, None),
        P("dp", "prec", None, None),
    )
    return jax.shard_map(
        shards,
        mesh=mesh,
        in_specs=placed,
        out_specs=(P("dp", "prec"), P("dp", "prec", None, None), P("dp", "prec", None, None)),
        check_vma=False,
    )
```

```python
import functools

import jax
import jax.numpy as jnp
from jax import lax
from jax.experimental import pallas as pl
from jax.experimental.pallas import tpu as pltpu
from jax.sharding import PartitionSpec as P

CAP = 2
HALVES = 2
SUBS = 2
TILE = 128
UNIT = 16
DECAY = 0.95
BF = jnp.bfloat16
F32 = jnp.float32


def nn(a, b):
    return jnp.dot(a, b, preferred_element_type=F32)


def nt(a, b):
    return lax.dot_general(a, b, (((1,), (1,)), ((), ())), preferred_element_type=F32)


def tn(a, b):
    return lax.dot_general(a, b, (((0,), (0,)), ((), ())), preferred_element_type=F32)


def upper_tiles(blk):
    side = blk // TILE
    return [(i, j) for i in range(side) for j in range(i, side)]


def five_minus(m):
    rows = lax.broadcasted_iota(jnp.int32, m.shape, 0)
    cols = lax.broadcasted_iota(jnp.int32, m.shape, 1)
    return jnp.where(rows == cols, 1.25, 0.0) - 0.25 * m


def inverse_root(a_ref, out_ref, f_ref):
    a = a_ref[...]
    top = jnp.max(jnp.sum(jnp.abs(a), axis=0, keepdims=True), axis=1, keepdims=True) + 1e-06
    z = 2.5 / top
    m0 = a * z
    m0b = m0.astype(BF)
    f0b = five_minus(m0).astype(BF)
    sq = nn(f0b, f0b).astype(BF)
    quad = nn(sq, sq).astype(BF)
    f_ref[...] = five_minus(nn(quad, m0b))
    f1b = f_ref[...].astype(BF)
    s1 = nn(f1b, f1b)
    u = (5.0 * f_ref[...] - 4.0 * s1).astype(BF)
    s1 = s1.astype(BF)
    q1 = nn(s1, s1).astype(BF)
    h = (1.25 * f_ref[...] - 0.25 * nn(q1, u)).astype(BF)
    out_ref[...] = (nn(f0b, h) * jnp.sqrt(jnp.sqrt(z))).astype(BF)


def travel_kernel(
    nd, npr,
    own_ref, act_ref, cot_ref, left_ref, right_ref,
    half_ref, xr_ref, slots_ref,
    a_all, cbuf, ct, stat, pk1, st1, pk2, st2, rs_out, rs_in, part, gt, gsa, gsb, g1a, g1b, pk3a, pk3b, sla, slb, mats, f_scr, xl,
    table,
    loc_sem, stat_sem, xs, xr, rss, rsr, s1s, s1r, s2s, s2r, g1s, g1r, g2s, g2r,
):
    nz = nd // 2
    arc = nz // 2
    tok, blk = cot_ref.shape
    hrow = blk // HALVES
    srow = hrow // SUBS
    grow = hrow // npr
    d = lax.axis_index("dp")
    p = lax.axis_index("prec")
    z = d // 2
    core = d % 2
    twin = d + 1 - 2 * core
    up = (d + 2) % nd
    down = (d + nd - 2) % nd
    MESH = pl.DeviceIdType.MESH
    g1 = (g1a, g1b)
    gs = (gsa, gsb)
    pk3 = (pk3a, pk3b)
    landed = (sla, slb)
    tiles = upper_tiles(blk)

    def remote(src, dst, ssem, rsem, **where):
        return pltpu.make_async_remote_copy(
            src_ref=src, dst_ref=dst, send_sem=ssem, recv_sem=rsem,
            device_id=where, device_id_type=MESH,
        )

    def peers(fn):
        @pl.loop(1, npr)
        def _(s):
            fn((p + s) % npr)

    def order(k):
        return (z + nz + (2 * (k % 2) - 1) * (arc - (k + 1) // 2)) % nz

    def own_rows(k):
        dest = order(k)
        cols = pl.ds(pl.multiple_of((2 * dest + core) * blk, blk), blk)
        return pltpu.make_async_copy(
            act_ref.at[:, cols], a_all.at[k, pl.ds(0, tok)], loc_sem.at[k]
        )

    def twin_rows(k):
        dest = order(k)
        cols = pl.ds(pl.multiple_of((2 * dest + 1 - core) * blk, blk), blk)
        return remote(
            act_ref.at[:, cols], a_all.at[k, pl.ds(tok, tok)], xs.at[k], xr.at[k], dp=twin
        )

    own_cot = pltpu.make_async_copy(cot_ref, cbuf.at[pl.ds(0, tok)], loc_sem.at[nz])
    twin_cot = remote(cot_ref, cbuf.at[pl.ds(tok, tok)], xs.at[nz], xr.at[nz], dp=twin)
    left_in = pltpu.make_async_copy(left_ref.at[0], stat.at[0], stat_sem.at[0])
    right_in = pltpu.make_async_copy(right_ref.at[0], stat.at[1], stat_sem.at[1])

    def make_table():
        @pl.loop(0, npr * CAP)
        def _(q):
            def pick(c, found):
                return jnp.where(own_ref[0, c] == q, c, found)

            table[q] = lax.fori_loop(0, npr, pick, jnp.int32(0))

    own_cot.start()

    @pl.loop(0, nz)
    def _(k):
        own_rows(k).start()

    left_in.start()
    right_in.start()

    barrier = pltpu.get_barrier_semaphore()
    for other in (twin, up, down):
        pl.semaphore_signal(barrier, inc=1, device_id={"dp": other}, device_id_type=MESH)
    peers(
        lambda t: pl.semaphore_signal(barrier, inc=1, device_id={"prec": t}, device_id_type=MESH)
    )
    make_table()
    pl.semaphore_wait(barrier, 3 + npr - 1)

    twin_cot.start()

    @pl.loop(0, nz)
    def _(k):
        twin_rows(k).start()

    def stat_one(t):
        return remote(
            pk1.at[t], st1.at[pl.ds(p * CAP, CAP)], s1s.at[t], s1r.at[p], prec=t
        )

    def stat_one_from(u):
        return remote(
            pk1.at[u], st1.at[pl.ds(u * CAP, CAP)], s1s.at[u], s1r.at[u], prec=u
        )

    def stat_two(t):
        return remote(pk2.at[t], st2.at[p], s2s.at[t], s2r.at[p], prec=t)

    def stat_two_from(u):
        return remote(pk2.at[u], st2.at[u], s2s.at[u], s2r.at[u], prec=u)

    def pack_stats():
        left_in.wait()
        right_in.wait()

        @pl.loop(0, CAP)
        def _(slot):
            for m in range(2):
                for n, (i, j) in enumerate(tiles):
                    for u in range(TILE // UNIT):
                        at = (m * len(tiles) + n) * (TILE // UNIT) + u
                        pk1[at % npr, slot, pl.ds(at // npr * UNIT, UNIT), :] = stat[
                            m, slot, pl.ds(i * TILE + u * UNIT, UNIT), pl.ds(j * TILE, TILE)
                        ].astype(BF)

    def turn_stats():
        peers(lambda u: stat_one_from(u).wait_recv())
        st1[pl.ds(p * CAP, CAP)] = pk1[p]

        @pl.loop(0, npr)
        def _(c):
            pk2[c] = st1[own_ref[0, c]]

        peers(lambda t: stat_two(t).start())

    def unpack_stats():
        peers(lambda u: stat_two_from(u).wait_recv())
        st2[p] = pk2[p]
        for m in range(2):
            for n, (i, j) in enumerate(tiles):
                rows = []
                for u in range(TILE // UNIT):
                    at = (m * len(tiles) + n) * (TILE // UNIT) + u
                    rows.append(st2[at % npr, pl.ds(at // npr * UNIT, UNIT), :])
                tile = jnp.concatenate(rows, axis=0).astype(F32) * DECAY
                mats[m, pl.ds(i * TILE, TILE), pl.ds(j * TILE, TILE)] = tile
                if i != j:
                    mats[m, pl.ds(j * TILE, TILE), pl.ds(i * TILE, TILE)] = tile.T

    def grad_one(h, t):
        return remote(
            gs[h].at[t], g1[h].at[p],
            g1s.at[h, t], g1r.at[h, p], prec=t,
        )

    def grad_one_from(h, u):
        return remote(
            gs[h].at[u], g1[h].at[u],
            g1s.at[h, u], g1r.at[h, u], prec=u,
        )

    def grad_two(h, t):
        return remote(
            pk3[h].at[t], landed[h].at[p],
            g2s.at[h, t], g2r.at[h, p], prec=t,
        )

    def grad_two_from(h, u):
        return remote(
            pk3[h].at[u], landed[h].at[u],
            g2s.at[h, u], g2r.at[h, u], prec=u,
        )

    def ring(it, way, sub):
        return remote(
            rs_out.at[it, way, sub], rs_in.at[it, way, sub],
            rss.at[it, way * SUBS + sub], rsr.at[it, way * SUBS + sub],
            dp=up if way == 0 else down,
        )

    def finish_half(h):
        base = h * hrow
        last = h * arc + arc - 1
        part[0] = nn(ct[pl.ds(base, hrow), :], a_all[nz - 1])
        for sub in range(SUBS):
            for way in range(2):
                ring(last, way, sub).wait_recv()
            done = (
                part[0, pl.ds(sub * srow, srow), :]
                + rs_in[last, 0, sub].astype(F32)
                + rs_in[last, 1, sub].astype(F32)
            ).astype(BF)
            gt[pl.ds(base + sub * srow, srow), :] = done
            gs[h][pl.ds(sub * srow // grow, srow // grow)] = done.reshape(
                srow // grow, grow, blk
            )
        peers(lambda t: grad_one(h, t).start())

    def turn_half(h):
        peers(lambda u: grad_one_from(h, u).wait_recv())
        g1[h][p] = gs[h][p]

        @pl.loop(0, npr)
        def _(o):
            for slot in range(CAP):
                pk3[h][o, slot] = g1[h][table[o * CAP + slot]]

        peers(lambda t: grad_two(h, t).start())

    def rows_ready(k):
        own_rows(k).wait()
        twin_rows(k).wait_recv()

    def far_end(way, sub):
        return (way == 0) == (sub < SUBS // 2)

    lanes = [(way, sub) for sub in range(SUBS) for way in range(2)]
    lanes.sort(key=lambda lane: far_end(*lane))

    def ring_step(h, s):
        it = h * arc + s
        mine = pl.ds(h * hrow, hrow)

        @pl.when(s == 0)
        def _():
            part[0] = nn(ct[mine, :], a_all[0])

        @pl.when(s > 0)
        def _():
            part[0] = nn(ct[mine, :], a_all[2 * s - 1])
            part[1] = nn(ct[mine, :], a_all[2 * s])

        for way, sub in lanes:
            rows = pl.ds(sub * srow, srow)
            begin = 0 if far_end(way, sub) else 1

            @pl.when(s == begin)
            def _():
                rs_out[it, way, sub] = part[begin * way, rows, :].astype(BF)
                ring(it, way, sub).start()

            @pl.when(s > begin)
            def _():
                ring(it - 1, way, sub).wait_recv()
                rs_out[it, way, sub] = (
                    part[way, rows, :] + rs_in[it - 1, way, sub].astype(F32)
                ).astype(BF)
                ring(it, way, sub).start()

    pack_stats()
    own_cot.wait()
    twin_cot.wait_recv()
    ct[...] = cbuf[...].T

    @pl.loop(0, arc + 2)
    def _(j):
        @pl.when((j > 0) & (j < arc))
        def _():
            rows_ready(2 * j - 1)

        @pl.when(j < arc)
        def _():
            rows_ready(2 * j)
            ring_step(0, j)

        @pl.when(j == 0)
        def _():
            peers(lambda t: stat_one(t).start())

        @pl.when(j == arc)
        def _():
            rows_ready(nz - 1)
            finish_half(0)

        @pl.when(j >= 2)
        def _():
            ring_step(1, j - 2)

        @pl.when(j == arc - 1)
        def _():
            turn_stats()

        @pl.when(j == arc + 1)
        def _():
            turn_half(0)

    finish_half(1)
    unpack_stats()
    g = gt[...]
    mats[1] += nt(g, g) * (1.0 / blk)
    inverse_root(mats.at[1], xr_ref, f_scr)
    turn_half(1)
    mats[0] += tn(g, g) * (1.0 / blk)
    inverse_root(mats.at[0], xl, f_scr)
    half_ref[...] = nt(xl[...], gt[...]).astype(BF)

    for h in range(HALVES):
        peers(lambda u, h=h: grad_two_from(h, u).wait_recv())
        landed[h][p] = pk3[h][p]
        slots_ref[h] = landed[h][...]

    twin_cot.wait_send()

    @pl.loop(0, nz)
    def _(k):
        twin_rows(k).wait_send()

    @pl.loop(0, HALVES * arc)
    def _(it):
        for way, sub in lanes:
            if far_end(way, sub):
                ring(it, way, sub).wait_send()
            else:

                @pl.when(it % arc > 0)
                def _():
                    ring(it, way, sub).wait_send()

    def sent(t):
        stat_one(t).wait_send()
        stat_two(t).wait_send()
        for h in range(HALVES):
            grad_one(h, t).wait_send()
            grad_two(h, t).wait_send()

    peers(sent)


def fresh_kernel(own_ref, half_ref, xr_ref, slots_ref, left_ref, right_ref,
                 upd_ref, lout_ref, rout_ref, stat, upd, out_sem):
    blk = xr_ref.shape[0]
    first = lax.axis_index("prec") * CAP
    stats_in, stats_out = (left_ref, right_ref), (lout_ref, rout_ref)
    quarter = blk // 2

    def store(slot, m, part):
        rows = pl.ds(part * quarter, quarter)
        return pltpu.make_async_copy(
            stat.at[slot, m, rows], stats_out[m].at[0, slot, rows],
            out_sem.at[(slot * 2 + m) * 2 + part],
        )

    upd_out = pltpu.make_async_copy(upd, upd_ref, out_sem.at[4 * CAP])
    upd[...] = nn(half_ref[...], xr_ref[...]).astype(BF)
    upd_out.start()
    for slot in range(CAP):
        named = jnp.int32(0)
        for c in range(own_ref.shape[1]):
            named = named + (own_ref[0, c] == first + slot).astype(jnp.int32)

        @pl.when(named > 0)
        def _():
            g = slots_ref[:, :, slot].reshape(blk, blk)
            for m, product in ((1, nt), (0, tn)):
                for part in range(2):
                    rows = slice(part * quarter, (part + 1) * quarter)
                    piece = g[rows, :] if m else g[:, rows]
                    stat[slot, m, rows] = DECAY * stats_in[m][0, slot, rows] + product(
                        piece, g
                    ) * (1.0 / blk)
                    store(slot, m, part).start()

        @pl.when(named == 0)
        def _():
            for m in range(2):
                stat[slot, m] = stats_in[m][0, slot]
                for part in range(2):
                    store(slot, m, part).start()

    upd_out.wait()
    for slot in range(CAP):
        for m in range(2):
            for part in range(2):
                store(slot, m, part).wait()


def in_hbm(array):
    return pltpu.with_memory_space_constraint(array, pltpu.HBM)


def shards(activations, cotangents, owner_slots, left_stats, right_stats):
    nd = lax.axis_size("dp")
    npr = lax.axis_size("prec")
    tok, blk = cotangents.shape
    nz = nd // 2
    its = HALVES * (nz // 2)
    hrow = blk // HALVES
    srow = hrow // SUBS
    grow = hrow // npr
    srows = 2 * len(upper_tiles(blk)) * TILE // npr
    dma = pltpu.SemaphoreType.DMA
    vmem = pl.BlockSpec(memory_space=pltpu.VMEM)
    far = pl.BlockSpec(memory_space=pltpu.HBM)
    half, xr, slots = pl.pallas_call(
        functools.partial(travel_kernel, nd, npr),
        out_shape=[
            jax.ShapeDtypeStruct((blk, blk), BF),
            jax.ShapeDtypeStruct((blk, blk), BF),
            jax.ShapeDtypeStruct((HALVES, npr, CAP, grow, blk), BF),
        ],
        in_specs=[pl.BlockSpec(memory_space=pltpu.SMEM)] + [far] * 4,
        out_specs=[vmem] * 3,
        scratch_shapes=[
            pltpu.VMEM((nz, 2 * tok, blk), BF),
            pltpu.VMEM((2 * tok, blk), BF),
            pltpu.VMEM((blk, 2 * tok), BF),
            pltpu.VMEM((2, CAP, blk, blk), F32),
            pltpu.VMEM((npr, CAP, srows, TILE), BF),
            pltpu.VMEM((npr * CAP, srows, TILE), BF),
            pltpu.VMEM((npr, srows, TILE), BF),
            pltpu.VMEM((npr, srows, TILE), BF),
            pltpu.VMEM((its, 2, SUBS, srow, blk), BF),
            pltpu.VMEM((its, 2, SUBS, srow, blk), BF),
            pltpu.VMEM((2, hrow, blk), F32),
            pltpu.VMEM((blk, blk), BF),
            pltpu.VMEM((npr, grow, blk), BF),
            pltpu.VMEM((npr, grow, blk), BF),
            pltpu.VMEM((npr, grow, blk), BF),
            pltpu.VMEM((npr, grow, blk), BF),
            pltpu.VMEM((npr, CAP, grow, blk), BF),
            pltpu.VMEM((npr, CAP, grow, blk), BF),
            pltpu.VMEM((npr, CAP, grow, blk), BF),
            pltpu.VMEM((npr, CAP, grow, blk), BF),
            pltpu.VMEM((2, blk, blk), F32),
            pltpu.VMEM((blk, blk), F32),
            pltpu.VMEM((blk, blk), BF),
            pltpu.SMEM((npr * CAP,), jnp.int32),
            dma((nz + 1,)),
            dma((2,)),
            dma((nz + 1,)),
            dma((nz + 1,)),
            dma((its, 2 * SUBS)),
            dma((its, 2 * SUBS)),
            dma((npr,)),
            dma((npr,)),
            dma((npr,)),
            dma((npr,)),
            dma((HALVES, npr)),
            dma((HALVES, npr)),
            dma((HALVES, npr)),
            dma((HALVES, npr)),
        ],
        compiler_params=pltpu.CompilerParams(
            collective_id=0, has_side_effects=True, vmem_limit_bytes=44 * 1024 * 1024
        ),
        name="travel",
    )(*[in_hbm(a) for a in (owner_slots, activations, cotangents, left_stats, right_stats)])

    update, left_out, right_out = pl.pallas_call(
        fresh_kernel,
        out_shape=[
            jax.ShapeDtypeStruct((blk, blk), BF),
            jax.ShapeDtypeStruct(left_stats.shape, F32),
            jax.ShapeDtypeStruct(right_stats.shape, F32),
        ],
        in_specs=[pl.BlockSpec(memory_space=pltpu.SMEM)] + [vmem] * 5,
        out_specs=[far] * 3,
        scratch_shapes=[
            pltpu.VMEM((CAP, 2, blk, blk), F32),
            pltpu.VMEM((blk, blk), BF),
            dma((4 * CAP + 1,)),
        ],
        compiler_params=pltpu.CompilerParams(vmem_limit_bytes=32 * 1024 * 1024),
        name="fresh",
    )(owner_slots, half, xr, slots, left_stats, right_stats)
    return (update, left_out, right_out)


def solution(mesh):
    placed = (
        P("dp", None),
        P("dp", "prec"),
        P("dp", None),
        P("dp", "prec", None, None),
        P("dp", "prec", None, None),
    )
    return jax.shard_map(
        shards,
        mesh=mesh,
        in_specs=placed,
        out_specs=(P("dp", "prec"), P("dp", "prec", None, None), P("dp", "prec", None, None)),
        check_vma=False,
    )
```

```python
import functools

import jax
import jax.numpy as jnp
from jax import lax
from jax.experimental import pallas as pl
from jax.experimental.pallas import tpu as pltpu
from jax.sharding import PartitionSpec as P

CAP = 2
HALVES = 2
SUBS = 2
TILE = 128
UNIT = 16
DECAY = 0.95
BF = jnp.bfloat16
F32 = jnp.float32


def nn(a, b):
    return jnp.dot(a, b, preferred_element_type=F32)


def nt(a, b):
    return lax.dot_general(a, b, (((1,), (1,)), ((), ())), preferred_element_type=F32)


def tn(a, b):
    return lax.dot_general(a, b, (((0,), (0,)), ((), ())), preferred_element_type=F32)


def upper_tiles(blk):
    side = blk // TILE
    return [(i, j) for i in range(side) for j in range(i, side)]


def five_minus(m):
    rows = lax.broadcasted_iota(jnp.int32, m.shape, 0)
    cols = lax.broadcasted_iota(jnp.int32, m.shape, 1)
    return jnp.where(rows == cols, 1.25, 0.0) - 0.25 * m


def inverse_root(a_ref, out_ref, f_ref):
    a = a_ref[...]
    top = jnp.max(jnp.sum(jnp.abs(a), axis=0, keepdims=True), axis=1, keepdims=True) + 1e-06
    z = 2.5 / top
    m0 = a * z
    m0b = m0.astype(BF)
    f0b = five_minus(m0).astype(BF)
    sq = nn(f0b, f0b).astype(BF)
    quad = nn(sq, sq).astype(BF)
    f_ref[...] = five_minus(nn(quad, m0b))
    f1b = f_ref[...].astype(BF)
    s1 = nn(f1b, f1b)
    u = (5.0 * f_ref[...] - 4.0 * s1).astype(BF)
    s1 = s1.astype(BF)
    q1 = nn(s1, s1).astype(BF)
    h = (1.25 * f_ref[...] - 0.25 * nn(q1, u)).astype(BF)
    out_ref[...] = (nn(f0b, h) * jnp.sqrt(jnp.sqrt(z))).astype(BF)


def travel_kernel(
    nd, npr,
    own_ref, act_ref, cot_ref, left_ref, right_ref,
    upd_ref, slots_ref,
    a_all, cbuf, ct, cx, stat, pk1, st1, pk2, st2, rs_out, rs_in, part, gt, gsa, gsb, g1a, g1b, pk3a, pk3b, sla, slb, mats, f_scr, xl, xr_ref,
    table,
    loc_sem, stat_sem, xs, xr, rss, rsr, s1s, s1r, s2s, s2r, g1s, g1r, g2s, g2r,
):
    nz = nd // 2
    arc = nz // 2
    tok, blk = cot_ref.shape
    hrow = blk // HALVES
    srow = hrow // SUBS
    grow = hrow // npr
    d = lax.axis_index("dp")
    p = lax.axis_index("prec")
    z = d // 2
    core = d % 2
    twin = d + 1 - 2 * core
    up = (d + 2) % nd
    down = (d + nd - 2) % nd
    MESH = pl.DeviceIdType.MESH
    g1 = (g1a, g1b)
    gs = (gsa, gsb)
    pk3 = (pk3a, pk3b)
    landed = (sla, slb)
    tiles = upper_tiles(blk)

    def remote(src, dst, ssem, rsem, **where):
        return pltpu.make_async_remote_copy(
            src_ref=src, dst_ref=dst, send_sem=ssem, recv_sem=rsem,
            device_id=where, device_id_type=MESH,
        )

    def peers(fn):
        @pl.loop(1, npr)
        def _(s):
            fn((p + s) % npr)

    def order(k):
        return (z + nz + (2 * (k % 2) - 1) * (arc - (k + 1) // 2)) % nz

    def own_rows(k):
        dest = order(k)
        cols = pl.ds(pl.multiple_of((2 * dest + core) * blk, blk), blk)
        return pltpu.make_async_copy(
            act_ref.at[:, cols], a_all.at[k, pl.ds(0, tok)], loc_sem.at[k]
        )

    def twin_rows(k):
        dest = order(k)
        cols = pl.ds(pl.multiple_of((2 * dest + 1 - core) * blk, blk), blk)
        return remote(
            act_ref.at[:, cols], a_all.at[k, pl.ds(tok, tok)], xs.at[k], xr.at[k], dp=twin
        )

    own_cot = pltpu.make_async_copy(cot_ref, cbuf, loc_sem.at[nz])
    twin_cot = remote(ct, cx, xs.at[nz], xr.at[nz], dp=twin)
    left_in = pltpu.make_async_copy(left_ref.at[0], stat.at[0], stat_sem.at[0])
    right_in = pltpu.make_async_copy(right_ref.at[0], stat.at[1], stat_sem.at[1])

    def make_table():
        @pl.loop(0, npr * CAP)
        def _(q):
            def pick(c, found):
                return jnp.where(own_ref[0, c] == q, c, found)

            table[q] = lax.fori_loop(0, npr, pick, jnp.int32(0))

    own_cot.start()

    @pl.loop(0, nz)
    def _(k):
        own_rows(k).start()

    left_in.start()
    right_in.start()

    barrier = pltpu.get_barrier_semaphore()
    for other in (twin, up, down):
        pl.semaphore_signal(barrier, inc=1, device_id={"dp": other}, device_id_type=MESH)
    peers(
        lambda t: pl.semaphore_signal(barrier, inc=1, device_id={"prec": t}, device_id_type=MESH)
    )
    own_cot.wait()
    ct[...] = cbuf[...].T
    make_table()
    pl.semaphore_wait(barrier, 3 + npr - 1)

    twin_cot.start()

    @pl.loop(0, nz)
    def _(k):
        twin_rows(k).start()

    def stat_one(t):
        return remote(
            pk1.at[t], st1.at[pl.ds(p * CAP, CAP)], s1s.at[t], s1r.at[p], prec=t
        )

    def stat_one_from(u):
        return remote(
            pk1.at[u], st1.at[pl.ds(u * CAP, CAP)], s1s.at[u], s1r.at[u], prec=u
        )

    def stat_two(t):
        return remote(pk2.at[t], st2.at[p], s2s.at[t], s2r.at[p], prec=t)

    def stat_two_from(u):
        return remote(pk2.at[u], st2.at[u], s2s.at[u], s2r.at[u], prec=u)

    def pack_stats():
        left_in.wait()
        right_in.wait()

        @pl.loop(0, CAP)
        def _(slot):
            for m in range(2):
                for n, (i, j) in enumerate(tiles):
                    for u in range(TILE // UNIT):
                        at = (m * len(tiles) + n) * (TILE // UNIT) + u
                        pk1[at % npr, slot, pl.ds(at // npr * UNIT, UNIT), :] = stat[
                            m, slot, pl.ds(i * TILE + u * UNIT, UNIT), pl.ds(j * TILE, TILE)
                        ].astype(BF)

    def turn_stats():
        peers(lambda u: stat_one_from(u).wait_recv())
        st1[pl.ds(p * CAP, CAP)] = pk1[p]

        @pl.loop(0, npr)
        def _(c):
            pk2[c] = st1[own_ref[0, c]]

        peers(lambda t: stat_two(t).start())

    def unpack_stats():
        peers(lambda u: stat_two_from(u).wait_recv())
        st2[p] = pk2[p]
        for m in range(2):
            for n, (i, j) in enumerate(tiles):
                rows = []
                for u in range(TILE // UNIT):
                    at = (m * len(tiles) + n) * (TILE // UNIT) + u
                    rows.append(st2[at % npr, pl.ds(at // npr * UNIT, UNIT), :])
                tile = jnp.concatenate(rows, axis=0).astype(F32) * DECAY
                mats[m, pl.ds(i * TILE, TILE), pl.ds(j * TILE, TILE)] = tile
                if i != j:
                    mats[m, pl.ds(j * TILE, TILE), pl.ds(i * TILE, TILE)] = tile.T

    def grad_one(h, t):
        return remote(
            gs[h].at[t], g1[h].at[p],
            g1s.at[h, t], g1r.at[h, p], prec=t,
        )

    def grad_one_from(h, u):
        return remote(
            gs[h].at[u], g1[h].at[u],
            g1s.at[h, u], g1r.at[h, u], prec=u,
        )

    def grad_two(h, t):
        return remote(
            pk3[h].at[t], landed[h].at[p],
            g2s.at[h, t], g2r.at[h, p], prec=t,
        )

    def grad_two_from(h, u):
        return remote(
            pk3[h].at[u], landed[h].at[u],
            g2s.at[h, u], g2r.at[h, u], prec=u,
        )

    def ring(it, way, sub):
        return remote(
            rs_out.at[it, way, sub], rs_in.at[it, way, sub],
            rss.at[it, way * SUBS + sub], rsr.at[it, way * SUBS + sub],
            dp=up if way == 0 else down,
        )

    def product(rows, k):
        return nn(ct[rows, :], a_all[k, pl.ds(0, tok)]) + nn(cx[rows, :], a_all[k, pl.ds(tok, tok)])

    def finish_half(h):
        base = h * hrow
        last = h * arc + arc - 1
        part[0] = product(pl.ds(base, hrow), nz - 1)
        for sub in range(SUBS):
            for way in range(2):
                ring(last, way, sub).wait_recv()
            done = (
                part[0, pl.ds(sub * srow, srow), :]
                + rs_in[last, 0, sub].astype(F32)
                + rs_in[last, 1, sub].astype(F32)
            ).astype(BF)
            gt[pl.ds(base + sub * srow, srow), :] = done
            gs[h][pl.ds(sub * srow // grow, srow // grow)] = done.reshape(
                srow // grow, grow, blk
            )
        peers(lambda t: grad_one(h, t).start())

    def turn_half(h):
        peers(lambda u: grad_one_from(h, u).wait_recv())
        g1[h][p] = gs[h][p]

        @pl.loop(0, npr)
        def _(o):
            for slot in range(CAP):
                pk3[h][o, slot] = g1[h][table[o * CAP + slot]]

        peers(lambda t: grad_two(h, t).start())

    def rows_ready(k):
        own_rows(k).wait()
        twin_rows(k).wait_recv()

    def far_end(way, sub):
        return (way == 0) == (sub < SUBS // 2)

    lanes = [(way, sub) for sub in range(SUBS) for way in range(2)]
    lanes.sort(key=lambda lane: far_end(*lane))

    def ring_step(h, s):
        it = h * arc + s
        mine = pl.ds(h * hrow, hrow)

        @pl.when(s == 0)
        def _():
            part[0] = product(mine, 0)

        @pl.when(s > 0)
        def _():
            part[0] = product(mine, 2 * s - 1)
            part[1] = product(mine, 2 * s)

        for way, sub in lanes:
            rows = pl.ds(sub * srow, srow)
            begin = 0 if far_end(way, sub) else 1

            @pl.when(s == begin)
            def _():
                rs_out[it, way, sub] = part[begin * way, rows, :].astype(BF)
                ring(it, way, sub).start()

            @pl.when(s > begin)
            def _():
                ring(it - 1, way, sub).wait_recv()
                rs_out[it, way, sub] = (
                    part[way, rows, :] + rs_in[it - 1, way, sub].astype(F32)
                ).astype(BF)
                ring(it, way, sub).start()

    pack_stats()
    peers(lambda t: stat_one(t).start())
    twin_cot.wait_recv()

    @pl.loop(0, arc + 3)
    def _(j):
        @pl.when((j > 0) & (j < arc))
        def _():
            rows_ready(2 * j - 1)

        @pl.when(j < arc)
        def _():
            rows_ready(2 * j)
            ring_step(0, j)

        @pl.when(j == arc)
        def _():
            rows_ready(nz - 1)
            finish_half(0)

        @pl.when(j >= 3)
        def _():
            ring_step(1, j - 3)

        @pl.when(j == arc - 1)
        def _():
            turn_stats()

        @pl.when(j == arc + 2)
        def _():
            turn_half(0)

    finish_half(1)
    unpack_stats()
    g = gt[...]
    mats[1] += nt(g, g) * (1.0 / blk)
    inverse_root(mats.at[1], xr_ref, f_scr)
    turn_half(1)
    mats[0] += tn(g, g) * (1.0 / blk)
    inverse_root(mats.at[0], xl, f_scr)
    half = nt(xl[...], gt[...]).astype(BF)
    upd_ref[...] = nn(half, xr_ref[...]).astype(BF)

    for h in range(HALVES):
        peers(lambda u, h=h: grad_two_from(h, u).wait_recv())
        landed[h][p] = pk3[h][p]
        slots_ref[h] = landed[h][...]

    twin_cot.wait_send()

    @pl.loop(0, nz)
    def _(k):
        twin_rows(k).wait_send()

    @pl.loop(0, HALVES * arc)
    def _(it):
        for way, sub in lanes:
            if far_end(way, sub):
                ring(it, way, sub).wait_send()
            else:

                @pl.when(it % arc > 0)
                def _():
                    ring(it, way, sub).wait_send()

    def sent(t):
        stat_one(t).wait_send()
        stat_two(t).wait_send()
        for h in range(HALVES):
            grad_one(h, t).wait_send()
            grad_two(h, t).wait_send()

    peers(sent)


def fresh_kernel(own_ref, prepared_ref, slots_ref, left_ref, right_ref,
                 upd_ref, lout_ref, rout_ref, stat, out_sem):
    blk = prepared_ref.shape[0]
    first = lax.axis_index("prec") * CAP
    stats_in, stats_out = (left_ref, right_ref), (lout_ref, rout_ref)
    quarter = blk // 2

    def store(slot, m, part):
        rows = pl.ds(part * quarter, quarter)
        return pltpu.make_async_copy(
            stat.at[slot, m, rows], stats_out[m].at[0, slot, rows],
            out_sem.at[(slot * 2 + m) * 2 + part],
        )

    upd_out = pltpu.make_async_copy(prepared_ref, upd_ref, out_sem.at[4 * CAP])
    upd_out.start()
    for slot in range(CAP):
        named = jnp.int32(0)
        for c in range(own_ref.shape[1]):
            named = named + (own_ref[0, c] == first + slot).astype(jnp.int32)

        @pl.when(named > 0)
        def _():
            g = slots_ref[:, :, slot].reshape(blk, blk)
            for m, product in ((1, nt), (0, tn)):
                for part in range(2):
                    rows = slice(part * quarter, (part + 1) * quarter)
                    piece = g[rows, :] if m else g[:, rows]
                    stat[slot, m, rows] = DECAY * stats_in[m][0, slot, rows] + product(
                        piece, g
                    ) * (1.0 / blk)
                    store(slot, m, part).start()

        @pl.when(named == 0)
        def _():
            for m in range(2):
                stat[slot, m] = stats_in[m][0, slot]
                for part in range(2):
                    store(slot, m, part).start()

    upd_out.wait()
    for slot in range(CAP):
        for m in range(2):
            for part in range(2):
                store(slot, m, part).wait()


def in_hbm(array):
    return pltpu.with_memory_space_constraint(array, pltpu.HBM)


def shards(activations, cotangents, owner_slots, left_stats, right_stats):
    nd = lax.axis_size("dp")
    npr = lax.axis_size("prec")
    tok, blk = cotangents.shape
    nz = nd // 2
    its = HALVES * (nz // 2)
    hrow = blk // HALVES
    srow = hrow // SUBS
    grow = hrow // npr
    srows = 2 * len(upper_tiles(blk)) * TILE // npr
    dma = pltpu.SemaphoreType.DMA
    vmem = pl.BlockSpec(memory_space=pltpu.VMEM)
    far = pl.BlockSpec(memory_space=pltpu.HBM)
    prepared, slots = pl.pallas_call(
        functools.partial(travel_kernel, nd, npr),
        out_shape=[
            jax.ShapeDtypeStruct((blk, blk), BF),
            jax.ShapeDtypeStruct((HALVES, npr, CAP, grow, blk), BF),
        ],
        in_specs=[pl.BlockSpec(memory_space=pltpu.SMEM)] + [far] * 4,
        out_specs=[vmem] * 2,
        scratch_shapes=[
            pltpu.VMEM((nz, 2 * tok, blk), BF),
            pltpu.VMEM((tok, blk), BF),
            pltpu.VMEM((blk, tok), BF),
            pltpu.VMEM((blk, tok), BF),
            pltpu.VMEM((2, CAP, blk, blk), F32),
            pltpu.VMEM((npr, CAP, srows, TILE), BF),
            pltpu.VMEM((npr * CAP, srows, TILE), BF),
            pltpu.VMEM((npr, srows, TILE), BF),
            pltpu.VMEM((npr, srows, TILE), BF),
            pltpu.VMEM((its, 2, SUBS, srow, blk), BF),
            pltpu.VMEM((its, 2, SUBS, srow, blk), BF),
            pltpu.VMEM((2, hrow, blk), F32),
            pltpu.VMEM((blk, blk), BF),
            pltpu.VMEM((npr, grow, blk), BF),
            pltpu.VMEM((npr, grow, blk), BF),
            pltpu.VMEM((npr, grow, blk), BF),
            pltpu.VMEM((npr, grow, blk), BF),
            pltpu.VMEM((npr, CAP, grow, blk), BF),
            pltpu.VMEM((npr, CAP, grow, blk), BF),
            pltpu.VMEM((npr, CAP, grow, blk), BF),
            pltpu.VMEM((npr, CAP, grow, blk), BF),
            pltpu.VMEM((2, blk, blk), F32),
            pltpu.VMEM((blk, blk), F32),
            pltpu.VMEM((blk, blk), BF),
            pltpu.VMEM((blk, blk), BF),
            pltpu.SMEM((npr * CAP,), jnp.int32),
            dma((nz + 1,)),
            dma((2,)),
            dma((nz + 1,)),
            dma((nz + 1,)),
            dma((its, 2 * SUBS)),
            dma((its, 2 * SUBS)),
            dma((npr,)),
            dma((npr,)),
            dma((npr,)),
            dma((npr,)),
            dma((HALVES, npr)),
            dma((HALVES, npr)),
            dma((HALVES, npr)),
            dma((HALVES, npr)),
        ],
        compiler_params=pltpu.CompilerParams(
            collective_id=0, has_side_effects=True, vmem_limit_bytes=44 * 1024 * 1024
        ),
        name="travel",
    )(*[in_hbm(a) for a in (owner_slots, activations, cotangents, left_stats, right_stats)])

    update, left_out, right_out = pl.pallas_call(
        fresh_kernel,
        out_shape=[
            jax.ShapeDtypeStruct((blk, blk), BF),
            jax.ShapeDtypeStruct(left_stats.shape, F32),
            jax.ShapeDtypeStruct(right_stats.shape, F32),
        ],
        in_specs=[pl.BlockSpec(memory_space=pltpu.SMEM)] + [vmem] * 4,
        out_specs=[far] * 3,
        scratch_shapes=[
            pltpu.VMEM((CAP, 2, blk, blk), F32),
            dma((4 * CAP + 1,)),
        ],
        compiler_params=pltpu.CompilerParams(vmem_limit_bytes=32 * 1024 * 1024),
        name="fresh",
    )(owner_slots, prepared, slots, left_stats, right_stats)
    return (update, left_out, right_out)


def solution(mesh):
    placed = (
        P("dp", None),
        P("dp", "prec"),
        P("dp", None),
        P("dp", "prec", None, None),
        P("dp", "prec", None, None),
    )
    return jax.shard_map(
        shards,
        mesh=mesh,
        in_specs=placed,
        out_specs=(P("dp", "prec"), P("dp", "prec", None, None), P("dp", "prec", None, None)),
        check_vma=False,
    )
```

```python
import functools

import jax
import jax.numpy as jnp
from jax import lax
from jax.experimental import pallas as pl
from jax.experimental.pallas import tpu as pltpu
from jax.sharding import PartitionSpec as P

CAP = 2
HALVES = 2
SUBS = 2
TILE = 128
UNIT = 16
DECAY = 0.95
BF = jnp.bfloat16
F32 = jnp.float32


def nn(a, b):
    return jnp.dot(a, b, preferred_element_type=F32)


def nt(a, b):
    return lax.dot_general(a, b, (((1,), (1,)), ((), ())), preferred_element_type=F32)


def tn(a, b):
    return lax.dot_general(a, b, (((0,), (0,)), ((), ())), preferred_element_type=F32)


def upper_tiles(blk):
    side = blk // TILE
    return [(i, j) for i in range(side) for j in range(i, side)]


def five_minus(m):
    rows = lax.broadcasted_iota(jnp.int32, m.shape, 0)
    cols = lax.broadcasted_iota(jnp.int32, m.shape, 1)
    return jnp.where(rows == cols, 1.25, 0.0) - 0.25 * m


def inverse_root(a_ref, out_ref, f_ref):
    a = a_ref[...]
    top = jnp.max(jnp.sum(jnp.abs(a), axis=0, keepdims=True), axis=1, keepdims=True) + 1e-06
    z = 2.5 / top
    m0 = a * z
    m0b = m0.astype(BF)
    f0b = five_minus(m0).astype(BF)
    sq = nn(f0b, f0b).astype(BF)
    quad = nn(sq, sq).astype(BF)
    f_ref[...] = five_minus(nn(quad, m0b))
    f1b = f_ref[...].astype(BF)
    s1 = nn(f1b, f1b)
    u = (5.0 * f_ref[...] - 4.0 * s1).astype(BF)
    s1 = s1.astype(BF)
    q1 = nn(s1, s1).astype(BF)
    h = (1.25 * f_ref[...] - 0.25 * nn(q1, u)).astype(BF)
    out_ref[...] = (nn(f0b, h) * jnp.sqrt(jnp.sqrt(z))).astype(BF)


def travel_kernel(
    nd, npr,
    own_ref, act_ref, cot_ref, left_ref, right_ref,
    upd_ref, slots_ref,
    a_all, cbuf, ct, cx, stat, pk1, st1, pk2, st2, rs_out, rs_in, part, gt, gsa, gsb, g1a, g1b, pk3a, pk3b, sla, slb, mats, f_scr, xl, xr_ref,
    table,
    loc_sem, stat_sem, xs, xr, rss, rsr, s1s, s1r, s2s, s2r, g1s, g1r, g2s, g2r,
):
    nz = nd // 2
    arc = nz // 2
    tok, blk = cot_ref.shape
    hrow = blk // HALVES
    srow = hrow // SUBS
    grow = hrow // npr
    d = lax.axis_index("dp")
    p = lax.axis_index("prec")
    z = d // 2
    core = d % 2
    twin = d + 1 - 2 * core
    up = (d + 2) % nd
    down = (d + nd - 2) % nd
    MESH = pl.DeviceIdType.MESH
    g1 = (g1a, g1b)
    gs = (gsa, gsb)
    pk3 = (pk3a, pk3b)
    landed = (sla, slb)
    tiles = upper_tiles(blk)

    def remote(src, dst, ssem, rsem, **where):
        return pltpu.make_async_remote_copy(
            src_ref=src, dst_ref=dst, send_sem=ssem, recv_sem=rsem,
            device_id=where, device_id_type=MESH,
        )

    def peers(fn):
        @pl.loop(1, npr)
        def _(s):
            fn((p + s) % npr)

    def order(k):
        return (z + nz + (2 * (k % 2) - 1) * (arc - (k + 1) // 2)) % nz

    def own_rows(k):
        dest = order(k)
        cols = pl.ds(pl.multiple_of((2 * dest + core) * blk, blk), blk)
        return pltpu.make_async_copy(
            act_ref.at[:, cols], a_all.at[k, pl.ds(0, tok)], loc_sem.at[k]
        )

    def twin_rows(k):
        dest = order(k)
        cols = pl.ds(pl.multiple_of((2 * dest + 1 - core) * blk, blk), blk)
        return remote(
            act_ref.at[:, cols], a_all.at[k, pl.ds(tok, tok)], xs.at[k], xr.at[k], dp=twin
        )

    own_cot = pltpu.make_async_copy(cot_ref, cbuf, loc_sem.at[nz])
    twin_cot = remote(ct, cx, xs.at[nz], xr.at[nz], dp=twin)
    left_in = pltpu.make_async_copy(left_ref.at[0], stat.at[0], stat_sem.at[0])
    right_in = pltpu.make_async_copy(right_ref.at[0], stat.at[1], stat_sem.at[1])

    def make_table():
        @pl.loop(0, npr * CAP)
        def _(q):
            def pick(c, found):
                return jnp.where(own_ref[0, c] == q, c, found)

            table[q] = lax.fori_loop(0, npr, pick, jnp.int32(0))

    own_cot.start()

    @pl.loop(0, nz)
    def _(k):
        own_rows(k).start()

    left_in.start()
    right_in.start()

    barrier = pltpu.get_barrier_semaphore()
    for other in (twin, up, down):
        pl.semaphore_signal(barrier, inc=1, device_id={"dp": other}, device_id_type=MESH)
    peers(
        lambda t: pl.semaphore_signal(barrier, inc=1, device_id={"prec": t}, device_id_type=MESH)
    )
    own_cot.wait()
    ct[...] = cbuf[...].T
    make_table()
    pl.semaphore_wait(barrier, 3 + npr - 1)

    twin_cot.start()

    @pl.loop(0, nz)
    def _(k):
        twin_rows(k).start()

    def stat_one(t):
        return remote(
            pk1.at[t], st1.at[pl.ds(p * CAP, CAP)], s1s.at[t], s1r.at[p], prec=t
        )

    def stat_one_from(u):
        return remote(
            pk1.at[u], st1.at[pl.ds(u * CAP, CAP)], s1s.at[u], s1r.at[u], prec=u
        )

    def stat_two(t):
        return remote(pk2.at[t], st2.at[p], s2s.at[t], s2r.at[p], prec=t)

    def stat_two_from(u):
        return remote(pk2.at[u], st2.at[u], s2s.at[u], s2r.at[u], prec=u)

    def pack_stats():
        left_in.wait()
        right_in.wait()

        @pl.loop(0, CAP)
        def _(slot):
            for m in range(2):
                for n, (i, j) in enumerate(tiles):
                    for u in range(TILE // UNIT):
                        at = (m * len(tiles) + n) * (TILE // UNIT) + u
                        pk1[at % npr, slot, pl.ds(at // npr * UNIT, UNIT), :] = stat[
                            m, slot, pl.ds(i * TILE + u * UNIT, UNIT), pl.ds(j * TILE, TILE)
                        ].astype(BF)

    def turn_stats():
        peers(lambda u: stat_one_from(u).wait_recv())
        st1[pl.ds(p * CAP, CAP)] = pk1[p]

        @pl.loop(0, npr)
        def _(c):
            pk2[c] = st1[own_ref[0, c]]

        peers(lambda t: stat_two(t).start())

    def unpack_stats():
        peers(lambda u: stat_two_from(u).wait_recv())
        st2[p] = pk2[p]
        for m in range(2):
            for n, (i, j) in enumerate(tiles):
                rows = []
                for u in range(TILE // UNIT):
                    at = (m * len(tiles) + n) * (TILE // UNIT) + u
                    rows.append(st2[at % npr, pl.ds(at // npr * UNIT, UNIT), :])
                tile = jnp.concatenate(rows, axis=0).astype(F32) * DECAY
                mats[m, pl.ds(i * TILE, TILE), pl.ds(j * TILE, TILE)] = tile
                if i != j:
                    mats[m, pl.ds(j * TILE, TILE), pl.ds(i * TILE, TILE)] = tile.T

    def grad_one(h, t):
        return remote(
            gs[h].at[t], g1[h].at[p],
            g1s.at[h, t], g1r.at[h, p], prec=t,
        )

    def grad_one_from(h, u):
        return remote(
            gs[h].at[u], g1[h].at[u],
            g1s.at[h, u], g1r.at[h, u], prec=u,
        )

    def grad_two(h, t):
        return remote(
            pk3[h].at[t], landed[h].at[p],
            g2s.at[h, t], g2r.at[h, p], prec=t,
        )

    def grad_two_from(h, u):
        return remote(
            pk3[h].at[u], landed[h].at[u],
            g2s.at[h, u], g2r.at[h, u], prec=u,
        )

    def ring(it, way, sub):
        return remote(
            rs_out.at[it, way, sub], rs_in.at[it, way, sub],
            rss.at[it, way * SUBS + sub], rsr.at[it, way * SUBS + sub],
            dp=up if way == 0 else down,
        )

    def product(rows, k):
        return nn(ct[rows, :], a_all[k, pl.ds(0, tok)]) + nn(cx[rows, :], a_all[k, pl.ds(tok, tok)])

    def finish_half(h):
        base = h * hrow
        last = h * arc + arc - 1
        part[0] = product(pl.ds(base, hrow), nz - 1)
        for sub in range(SUBS):
            for way in range(2):
                ring(last, way, sub).wait_recv()
            done = (
                part[0, pl.ds(sub * srow, srow), :]
                + rs_in[last, 0, sub].astype(F32)
                + rs_in[last, 1, sub].astype(F32)
            ).astype(BF)
            gt[pl.ds(base + sub * srow, srow), :] = done
            gs[h][pl.ds(sub * srow // grow, srow // grow)] = done.reshape(
                srow // grow, grow, blk
            )
        peers(lambda t: grad_one(h, t).start())

    def turn_half(h):
        peers(lambda u: grad_one_from(h, u).wait_recv())
        g1[h][p] = gs[h][p]

        @pl.loop(0, npr)
        def _(o):
            for slot in range(CAP):
                pk3[h][o, slot] = g1[h][table[o * CAP + slot]]

        peers(lambda t: grad_two(h, t).start())

    def rows_ready(k):
        own_rows(k).wait()
        twin_rows(k).wait_recv()

    def far_end(way, sub):
        return (way == 0) == (sub < SUBS // 2)

    lanes = [(way, sub) for sub in range(SUBS) for way in range(2)]
    lanes.sort(key=lambda lane: far_end(*lane))

    def ring_step(h, s):
        it = h * arc + s
        mine = pl.ds(h * hrow, hrow)

        @pl.when(s == 0)
        def _():
            part[0] = product(mine, 0)

        @pl.when(s > 0)
        def _():
            part[0] = product(mine, 2 * s - 1)
            part[1] = product(mine, 2 * s)

        for way, sub in lanes:
            rows = pl.ds(sub * srow, srow)
            begin = 0 if far_end(way, sub) else 1

            @pl.when(s == begin)
            def _():
                rs_out[it, way, sub] = part[begin * way, rows, :].astype(BF)
                ring(it, way, sub).start()

            @pl.when(s > begin)
            def _():
                ring(it - 1, way, sub).wait_recv()
                rs_out[it, way, sub] = (
                    part[way, rows, :] + rs_in[it - 1, way, sub].astype(F32)
                ).astype(BF)
                ring(it, way, sub).start()

    pack_stats()
    peers(lambda t: stat_one(t).start())
    twin_cot.wait_recv()

    @pl.loop(0, arc + 3)
    def _(j):
        @pl.when((j > 0) & (j < arc))
        def _():
            rows_ready(2 * j - 1)

        @pl.when(j < arc)
        def _():
            rows_ready(2 * j)
            ring_step(0, j)

        @pl.when(j == arc)
        def _():
            rows_ready(nz - 1)
            finish_half(0)

        @pl.when(j >= 3)
        def _():
            ring_step(1, j - 3)

        @pl.when(j == arc - 1)
        def _():
            turn_stats()

        @pl.when(j == arc + 1)
        def _():
            turn_half(0)

    finish_half(1)
    unpack_stats()
    g = gt[...]
    mats[1] += nt(g, g) * (1.0 / blk)
    inverse_root(mats.at[1], xr_ref, f_scr)
    turn_half(1)
    mats[0] += tn(g, g) * (1.0 / blk)
    inverse_root(mats.at[0], xl, f_scr)
    half = nt(xl[...], gt[...]).astype(BF)
    upd_ref[...] = nn(half, xr_ref[...]).astype(BF)

    for h in range(HALVES):
        peers(lambda u, h=h: grad_two_from(h, u).wait_recv())
        landed[h][p] = pk3[h][p]
        slots_ref[h] = landed[h][...]

    twin_cot.wait_send()

    @pl.loop(0, nz)
    def _(k):
        twin_rows(k).wait_send()

    @pl.loop(0, HALVES * arc)
    def _(it):
        for way, sub in lanes:
            if far_end(way, sub):
                ring(it, way, sub).wait_send()
            else:

                @pl.when(it % arc > 0)
                def _():
                    ring(it, way, sub).wait_send()

    def sent(t):
        stat_one(t).wait_send()
        stat_two(t).wait_send()
        for h in range(HALVES):
            grad_one(h, t).wait_send()
            grad_two(h, t).wait_send()

    peers(sent)


def fresh_kernel(own_ref, prepared_ref, slots_ref, left_ref, right_ref,
                 upd_ref, lout_ref, rout_ref, stat, out_sem):
    blk = prepared_ref.shape[0]
    first = lax.axis_index("prec") * CAP
    stats_in, stats_out = (left_ref, right_ref), (lout_ref, rout_ref)
    quarter = blk // 2

    def store(slot, m, part):
        rows = pl.ds(part * quarter, quarter)
        return pltpu.make_async_copy(
            stat.at[slot, m, rows], stats_out[m].at[0, slot, rows],
            out_sem.at[(slot * 2 + m) * 2 + part],
        )

    upd_out = pltpu.make_async_copy(prepared_ref, upd_ref, out_sem.at[4 * CAP])
    upd_out.start()
    for slot in range(CAP):
        named = jnp.int32(0)
        for c in range(own_ref.shape[1]):
            named = named + (own_ref[0, c] == first + slot).astype(jnp.int32)

        @pl.when(named > 0)
        def _():
            g = slots_ref[:, :, slot].reshape(blk, blk)
            for m, product in ((1, nt), (0, tn)):
                for part in range(2):
                    rows = slice(part * quarter, (part + 1) * quarter)
                    piece = g[rows, :] if m else g[:, rows]
                    stat[slot, m, rows] = DECAY * stats_in[m][0, slot, rows] + product(
                        piece, g
                    ) * (1.0 / blk)
                    store(slot, m, part).start()

        @pl.when(named == 0)
        def _():
            for m in range(2):
                stat[slot, m] = stats_in[m][0, slot]
                for part in range(2):
                    store(slot, m, part).start()

    upd_out.wait()
    for slot in range(CAP):
        for m in range(2):
            for part in range(2):
                store(slot, m, part).wait()


def in_hbm(array):
    return pltpu.with_memory_space_constraint(array, pltpu.HBM)


def shards(activations, cotangents, owner_slots, left_stats, right_stats):
    nd = lax.axis_size("dp")
    npr = lax.axis_size("prec")
    tok, blk = cotangents.shape
    nz = nd // 2
    its = HALVES * (nz // 2)
    hrow = blk // HALVES
    srow = hrow // SUBS
    grow = hrow // npr
    srows = 2 * len(upper_tiles(blk)) * TILE // npr
    dma = pltpu.SemaphoreType.DMA
    vmem = pl.BlockSpec(memory_space=pltpu.VMEM)
    far = pl.BlockSpec(memory_space=pltpu.HBM)
    prepared, slots = pl.pallas_call(
        functools.partial(travel_kernel, nd, npr),
        out_shape=[
            jax.ShapeDtypeStruct((blk, blk), BF),
            jax.ShapeDtypeStruct((HALVES, npr, CAP, grow, blk), BF),
        ],
        in_specs=[pl.BlockSpec(memory_space=pltpu.SMEM)] + [far] * 4,
        out_specs=[vmem] * 2,
        scratch_shapes=[
            pltpu.VMEM((nz, 2 * tok, blk), BF),
            pltpu.VMEM((tok, blk), BF),
            pltpu.VMEM((blk, tok), BF),
            pltpu.VMEM((blk, tok), BF),
            pltpu.VMEM((2, CAP, blk, blk), F32),
            pltpu.VMEM((npr, CAP, srows, TILE), BF),
            pltpu.VMEM((npr * CAP, srows, TILE), BF),
            pltpu.VMEM((npr, srows, TILE), BF),
            pltpu.VMEM((npr, srows, TILE), BF),
            pltpu.VMEM((its, 2, SUBS, srow, blk), BF),
            pltpu.VMEM((its, 2, SUBS, srow, blk), BF),
            pltpu.VMEM((2, hrow, blk), F32),
            pltpu.VMEM((blk, blk), BF),
            pltpu.VMEM((npr, grow, blk), BF),
            pltpu.VMEM((npr, grow, blk), BF),
            pltpu.VMEM((npr, grow, blk), BF),
            pltpu.VMEM((npr, grow, blk), BF),
            pltpu.VMEM((npr, CAP, grow, blk), BF),
            pltpu.VMEM((npr, CAP, grow, blk), BF),
            pltpu.VMEM((npr, CAP, grow, blk), BF),
            pltpu.VMEM((npr, CAP, grow, blk), BF),
            pltpu.VMEM((2, blk, blk), F32),
            pltpu.VMEM((blk, blk), F32),
            pltpu.VMEM((blk, blk), BF),
            pltpu.VMEM((blk, blk), BF),
            pltpu.SMEM((npr * CAP,), jnp.int32),
            dma((nz + 1,)),
            dma((2,)),
            dma((nz + 1,)),
            dma((nz + 1,)),
            dma((its, 2 * SUBS)),
            dma((its, 2 * SUBS)),
            dma((npr,)),
            dma((npr,)),
            dma((npr,)),
            dma((npr,)),
            dma((HALVES, npr)),
            dma((HALVES, npr)),
            dma((HALVES, npr)),
            dma((HALVES, npr)),
        ],
        compiler_params=pltpu.CompilerParams(
            collective_id=0, has_side_effects=True, vmem_limit_bytes=44 * 1024 * 1024
        ),
        name="travel",
    )(*[in_hbm(a) for a in (owner_slots, activations, cotangents, left_stats, right_stats)])

    update, left_out, right_out = pl.pallas_call(
        fresh_kernel,
        out_shape=[
            jax.ShapeDtypeStruct((blk, blk), BF),
            jax.ShapeDtypeStruct(left_stats.shape, F32),
            jax.ShapeDtypeStruct(right_stats.shape, F32),
        ],
        in_specs=[pl.BlockSpec(memory_space=pltpu.SMEM)] + [vmem] * 4,
        out_specs=[far] * 3,
        scratch_shapes=[
            pltpu.VMEM((CAP, 2, blk, blk), F32),
            dma((4 * CAP + 1,)),
        ],
        compiler_params=pltpu.CompilerParams(vmem_limit_bytes=32 * 1024 * 1024),
        name="fresh",
    )(owner_slots, prepared, slots, left_stats, right_stats)
    return (update, left_out, right_out)


def solution(mesh):
    placed = (
        P("dp", None),
        P("dp", "prec"),
        P("dp", None),
        P("dp", "prec", None, None),
        P("dp", "prec", None, None),
    )
    return jax.shard_map(
        shards,
        mesh=mesh,
        in_specs=placed,
        out_specs=(P("dp", "prec"), P("dp", "prec", None, None), P("dp", "prec", None, None)),
        check_vma=False,
    )
```
